128 devices in a mesh: comp: 8 (over z, core), lat: 16 (over y, x).
Axes of the slice: x: 4, y: 4, z: 4, core: 2. Of those that a mesh axis runs over, the one named last changes fastest.
Arguments:
- energy: float32 [1800, 64, 1536], P('comp', 'lat'), may hold values from 0.05 to 1
- sea_mask: int32 [64, 1536], replicated, may hold values from 0 to 1, as said below
- depth_class: int32 [64, 1536], replicated, may hold values from 0 to 7
- group_speed: float32 [50, 8], replicated, may hold values from 0.08 to 0.6
- wind_input: float32 [1800], replicated, may hold values from 0.05 to 0.5
- whitecap: float32 [1800], replicated, may hold values from 0.2 to 1
- pair_in: bfloat16 [1800, 1800], replicated, may hold values from -0.125 to 0.125
- pair_out: bfloat16 [1800, 1800], replicated, may hold values from -0.125 to 0.125
Outputs:
- energy_next: float32 [1800, 64, 1536], P('comp', 'lat')
The draws below stay inside these ranges and needn't reach their ends.
Inputs may be any that keep to these rules, and one draw needn't show every extreme that they name: `sea_mask`: cut every tile of 4 latitude rows into consecutive slices of 48 cells in row-major order; the slices at one slice position in all tiles together hold exactly 336 sea cells.
All inputs are finite; a program needn't handle non-finite values.
Results may differ from the reference program's by a relative error of at most 0.00065.
Values sent between devices are 32-bit elements; how exact they have to be, the bound alone decides.
A program may use at most 192 MiB of HBM per device.

```python
import math
import jax
import jax.numpy as jnp
from jax import lax

NFREQ = 50
NDIR = 36
K = 1800
NCLASS = 8
SUB = 2
NLON = 1536
NLAT = 64
SLICE = 48
N_COMP = 8
N_LAT = 16


def draw_sea_mask(key, part):
    key_rank, key_jitter, key_place = jax.random.split(key, 3)
    stride = 3 * SLICE // 4 // (N_LAT - 1)
    ranking = jax.random.permutation(key_rank, N_LAT)
    baseline = SLICE // 8 + stride * ranking
    jitter = jax.random.randint(key_jitter, (N_LAT, N_COMP * N_LAT), 0, SLICE // 16 + 1)
    counts = baseline[:, None] + jitter - jnp.roll(jitter, -1, axis=0)
    scores = jax.random.randint(key_place, (N_LAT, N_COMP * N_LAT, SLICE), 0, 65536) * SLICE + jnp.arange(SLICE)
    placing = jnp.argsort(jnp.argsort(scores, axis=-1, stable=True), axis=-1, stable=True)
    flags = (placing < counts[:, :, None]).astype(jnp.int32)
    return flags.reshape(NLAT, NLON)


def with_ends(result, own_key, smallest, top_value):
    place = [jax.random.randint(jax.random.fold_in(own_key, axis), (), 0, length) for axis, length in enumerate(result.shape)]
    longest = result.shape.index(max(result.shape))
    next_to = place[:longest] + [(place[longest] + 1) % result.shape[longest]] + place[longest + 1:]
    return result.at[tuple(place)].set(smallest).at[tuple(next_to)].set(top_value)


def block_scale(rng, dims, shards, smallest, largest):
    factor_of, own = 1.0, jax.random.fold_in(rng, 6)
    for axis_at, blocks in shards:
        draws = jnp.exp(jax.random.uniform(jax.random.fold_in(own, axis_at), (blocks,), jnp.float32, smallest / len(shards), largest / len(shards)))
        factor_of = factor_of * jnp.repeat(draws, dims[axis_at] // blocks).reshape([-1 if axis == axis_at else 1 for axis in range(len(dims))])
    return factor_of


def centred(own_key, extent, deviation, limit, held_as=jnp.bfloat16):
    return jnp.clip(deviation * jax.random.normal(own_key, extent, jnp.float32), -limit, limit).astype(held_as)


def setup_inputs(seed: int = 0) -> dict:
    splits = jax.random.split(jax.random.key(seed), 9)
    energy = jnp.clip(jnp.exp(math.log(1.0) - 2.9957323 * jax.random.uniform(splits[0], (K, NLAT, NLON), jnp.float32) ** block_scale(splits[0], (K, NLAT, NLON), ((0, 8), (1, 16)), -0.2, 0.2)), 0.05, 1.0)
    sea_mask = draw_sea_mask(jax.random.fold_in(splits[8], 71), 0)
    depth_class = with_ends(jax.random.randint(splits[2], (NLAT, NLON), 0, NCLASS), jax.random.fold_in(splits[2], 1), 0, NCLASS - 1).astype(jnp.int32)
    group_speed = jnp.clip(jnp.exp(jax.random.uniform(splits[3], (NFREQ, NCLASS), jnp.float32, math.log(0.08), math.log(0.6))), 0.08, 0.6)
    wind_input = jnp.clip(jnp.exp(jax.random.uniform(splits[4], (K,), jnp.float32, math.log(0.05), math.log(0.5))), 0.05, 0.5)
    whitecap = jnp.clip(jnp.exp(jax.random.uniform(splits[5], (K,), jnp.float32, math.log(0.2), math.log(1.0))), 0.2, 1.0)
    pair_in = centred(splits[6], (K, K), K ** -0.5, 0.125)
    pair_out = centred(splits[7], (K, K), K ** -0.5, 0.125)
    return {"energy": energy, "sea_mask": sea_mask, "depth_class": depth_class, "group_speed": group_speed, "wind_input": wind_input, "whitecap": whitecap, "pair_in": pair_in, "pair_out": pair_out}


time_step = 0.5


def advect(spectra, zonal_speed, meridional, sea_cells):
    padded = jnp.pad(spectra, ((0, 0), (1, 1), (1, 1)))
    south_cells = padded[:, :-2, 1:-1]
    north_cells = padded[:, 2:, 1:-1]
    west_cells = padded[:, 1:-1, :-2]
    east_cells = padded[:, 1:-1, 2:]
    advected = spectra - jnp.maximum(zonal_speed, 0.0) * (spectra - west_cells) - jnp.minimum(zonal_speed, 0.0) * (east_cells - spectra)
    advected = advected - jnp.maximum(meridional, 0.0) * (spectra - south_cells) - jnp.minimum(meridional, 0.0) * (north_cells - spectra)
    return advected * sea_cells


def source_terms(advected, pair_in, pair_out, wind_rate, white_rate):
    projected = jnp.dot(pair_in, advected.astype(jnp.bfloat16), preferred_element_type=jnp.float32)
    pair_terms = (projected * advected).astype(jnp.bfloat16)
    transfer = jnp.dot(pair_out, pair_terms, preferred_element_type=jnp.float32)
    mean_energy = jnp.mean(advected, axis=0, keepdims=True)
    return advected + time_step * (wind_rate[:, None] * advected - white_rate[:, None] * mean_energy * advected + transfer)


def reference(energy, sea_mask, depth_class, group_speed, wind_input, whitecap, pair_in, pair_out):
    sea_cells = sea_mask.astype(jnp.float32)
    angles = 2.0 * math.pi * (jnp.arange(NDIR).astype(jnp.float32) + 0.5) / NDIR
    cosine = jnp.cos(angles)
    sine_dir = jnp.sin(angles)
    grouped = energy.reshape(NFREQ, NDIR, NLAT, NLON)

    def propagate(inputs):
        spectra, speed_row = inputs
        speed_cells = speed_row[depth_class]
        zonal_speed = speed_cells[None] * cosine[:, None, None]
        meridional = speed_cells[None] * sine_dir[:, None, None]
        spectra = spectra * sea_cells
        for substep in range(SUB):
            spectra = advect(spectra, zonal_speed, meridional, sea_cells)
        return spectra

    advected = lax.map(propagate, (grouped, group_speed)).reshape(K, NLAT, NLON)
    rows_first = jnp.transpose(advected, (1, 0, 2))

    def source(column):
        return source_terms(column, pair_in, pair_out, wind_input, whitecap)

    updated = lax.map(source, rows_first)
    return jnp.transpose(updated, (1, 0, 2))
```

```python
import math

import jax
import jax.numpy as jnp
from jax import lax
from jax.experimental import pallas as pl
from jax.experimental.pallas import tpu as pltpu
from jax.sharding import PartitionSpec as P

NDIR = 36
SUB = 2
MESH = pl.DeviceIdType.MESH
F32 = jnp.float32
BF16 = jnp.bfloat16

time_step = 0.5

LANE = 128
CHUNK = 256
RUN = 18


def sections(lon):
    tiles, step = lon // LANE, CHUNK // LANE
    ends = [0] + [min(step * (q + 1) + 1, tiles) for q in range(lon // CHUNK)]
    return [(low, high - low) for low, high in zip(ends, ends[1:])]


def make_kernel(comp_count, lat_count, comp_local, rows, lon):
    chunks = lon // CHUNK
    total = comp_count * comp_local
    parts = sections(lon)
    window = CHUNK + 2 * LANE
    groups = comp_local // 8
    runs = comp_local // RUN
    rest = comp_local - runs * RUN
    row_tiles = [(0, 448), (448, 448), (896, 448), (1344, total - 1344)]

    def kernel(
        energy,
        pair_in,
        pair_out,
        sea,
        classes,
        table,
        rates,
        out,
        cells,
        halo,
        advected,
        gathered,
        returned,
        map_in,
        map_out,
        half,
        terms,
        load_sem,
        map_sem,
        halo_send,
        halo_recv,
        there_send,
        there_recv,
        back_send,
        back_recv,
        out_sem,
    ):
        c = lax.axis_index("comp")
        l = lax.axis_index("lat")
        odd = lax.rem(c, 2)

        def own(low, size):
            return pl.ds(low + 1, size)

        for q, (low, size) in enumerate(parts):
            for tile in range(low, low + size):
                for r in range(rows):
                    pltpu.make_async_copy(
                        energy.at[:, r, pl.ds(tile * LANE, LANE)],
                        cells.at[tile + 1, r],
                        load_sem.at[q],
                    ).start()

        barrier = pltpu.get_barrier_semaphore()
        north = lax.rem(l + 1, lat_count)
        south = lax.rem(l + lat_count - 1, lat_count)
        for d in range(1, comp_count):
            pl.semaphore_signal(
                barrier, inc=1, device_id=(lax.rem(c + d, comp_count), l), device_id_type=MESH
            )
        for other in (north, south):
            pl.semaphore_signal(barrier, inc=1, device_id=(c, other), device_id_type=MESH)
        pl.semaphore_wait(barrier, comp_count + 1)

        def send_halo(start, count, up, q):
            low, size = parts[q]
            for near in range(2):
                for is_up in (True, False):

                    @pl.when(up if is_up else jnp.logical_not(up))
                    def _():
                        pltpu.make_async_remote_copy(
                            src_ref=cells.at[
                                own(low, size),
                                rows - 1 - near if is_up else near,
                                pl.ds(start, count),
                            ],
                            dst_ref=halo.at[own(low, size), near, pl.ds(start, count)],
                            send_sem=halo_send.at[q],
                            recv_sem=halo_recv.at[q],
                            device_id=(c, north if is_up else south),
                            device_id_type=MESH,
                        ).start()

        for q, (low, size) in enumerate(parts):
            part = cells.at[own(low, size)]
            pltpu.make_async_copy(part, part, load_sem.at[q]).wait()

            @pl.loop(0, runs)
            def _(m):
                up = lax.rem((c + odd) // 2 + m, 2) == 0
                send_halo(m * RUN + odd * rest, RUN, up, q)

            send_halo((1 - odd) * runs * RUN, rest, lax.rem(c, 4) < 2, q)

        pltpu.make_async_copy(pair_in, map_in, map_sem.at[0]).start()
        pltpu.make_async_copy(pair_out, map_out, map_sem.at[1]).start()

        def advect_group(q, start):
            here = pl.ds(start, 8)
            lanes = pl.ds(pl.multiple_of(q * CHUNK, LANE), window)
            wide = (8, window)
            facts = table[here, :]
            tile = q * (CHUNK // LANE)

            def strip(ref, i):
                return jnp.concatenate(
                    [ref[tile + t, i, here, :] for t in range(window // LANE)], axis=1
                )

            def column(j):
                return jnp.broadcast_to(facts[:, j : j + 1], wide)

            cosine, sine = column(8), column(9)
            up = sine > 0.0
            eastward = cosine > 0.0

            def sea_row(i):
                return jnp.broadcast_to(sea[pl.ds(i, 1), lanes], wide)

            def class_row(i):
                return jnp.broadcast_to(classes[pl.ds(i, 1), lanes], wide)

            speeds = [column(j) for j in range(8)]

            def rates_of(kinds):
                speed = speeds[0]
                for level in range(1, 8):
                    speed = jnp.where(kinds == level, speeds[level], speed)
                return jnp.abs(speed * cosine), jnp.abs(speed * sine)

            def beside(v):
                return jnp.where(eastward, pltpu.roll(v, 1, 1), pltpu.roll(v, window - 1, 1))

            def moved(v, along, across, zonal, meridional, wet):
                return (v - zonal * (v - along) - meridional * (v - across)) * wet

            wet = [sea_row(i + 2) for i in range(rows)]
            wet_near = jnp.where(up, sea_row(1), sea_row(6))
            wet_far = jnp.where(up, sea_row(0), sea_row(7))
            e = [jnp.where(wet[i] > 0.0, strip(cells, i), 0.0) for i in range(rows)]
            near = jnp.where(wet_near > 0.0, strip(halo, 0), 0.0)
            far = jnp.where(wet_far > 0.0, strip(halo, 1), 0.0)
            speed_of = [rates_of(class_row(i + 2)) for i in range(rows)]
            near_speed = rates_of(jnp.where(up, class_row(1), class_row(6)))

            def across(v, edge, i):
                before = edge if i == 0 else v[i - 1]
                after = edge if i == rows - 1 else v[i + 1]
                return jnp.where(up, before, after)

            first = [
                moved(e[i], beside(e[i]), across(e, near, i), *speed_of[i], wet[i])
                for i in range(rows)
            ]
            first_near = moved(near, beside(near), far, *near_speed, wet_near)
            for i in range(rows):
                second = moved(
                    first[i], beside(first[i]), across(first, first_near, i), *speed_of[i], wet[i]
                )
                for t in range(CHUNK // LANE):
                    advected[q * comp_count + i * 2 + t, here, :] = second[
                        :, LANE * (t + 1) : LANE * (t + 2)
                    ]

        def wait_part(q):
            for k, (low, size) in enumerate(parts):

                @pl.when(q == k)
                def _():
                    part = halo.at[own(low, size)]
                    pltpu.make_async_copy(part, part, halo_recv.at[k]).wait()

        @pl.loop(0, chunks)
        def _(q):
            wait_part(q)

            @pl.loop(0, groups)
            def _(g):
                advect_group(q, pl.multiple_of(g * 8, 8))

            advect_group(q, comp_local - 8)

            place = gathered.at[q, pl.ds(c * comp_local, comp_local)]
            pltpu.make_async_copy(advected.at[q * comp_count + c], place, there_recv.at[q]).start()

            @pl.loop(1, comp_count)
            def _(d):
                home = lax.rem(c + d, comp_count)
                pltpu.make_async_remote_copy(
                    src_ref=advected.at[q * comp_count + home],
                    dst_ref=place,
                    send_sem=there_send.at[q],
                    recv_sem=there_recv.at[q],
                    device_id=(home, l),
                    device_id_type=MESH,
                ).start()

        pltpu.make_async_copy(pair_in, map_in, map_sem.at[0]).wait()
        pltpu.make_async_copy(pair_out, map_out, map_sem.at[1]).wait()

        @pl.loop(0, chunks)
        def _(q):
            pltpu.make_async_copy(gathered.at[q], gathered.at[q], there_recv.at[q]).wait()
            spectra = gathered[q]
            half[...] = spectra.astype(BF16)
            mean_energy = jnp.sum(spectra, axis=0, keepdims=True) * (1.0 / total)
            for low, size in row_tiles:
                projected = jnp.dot(
                    map_in[low : low + size, :], half[...], preferred_element_type=F32
                )
                terms[low : low + size, :] = (
                    projected * gathered[q, low : low + size, :]
                ).astype(BF16)
            for low, size in row_tiles:
                transfer = jnp.dot(
                    map_out[low : low + size, :], terms[...], preferred_element_type=F32
                )
                now = gathered[q, low : low + size, :]
                wind = rates[low : low + size, 0:1]
                white = rates[low : low + size, 1:2]
                gathered[q, low : low + size, :] = now + time_step * (
                    wind * now - white * mean_energy * now + transfer
                )

            place = returned.at[q * comp_count + c]
            pltpu.make_async_copy(
                gathered.at[q, pl.ds(c * comp_local, comp_local)], place, back_recv.at[q]
            ).start()

            @pl.loop(1, comp_count)
            def _(d):
                origin = lax.rem(c + d, comp_count)
                pltpu.make_async_remote_copy(
                    src_ref=gathered.at[q, pl.ds(origin * comp_local, comp_local)],
                    dst_ref=place,
                    send_sem=back_send.at[q],
                    recv_sem=back_recv.at[q],
                    device_id=(origin, l),
                    device_id_type=MESH,
                ).start()

        def write(q, i, t):
            b = q * comp_count + i * 2 + t
            return pltpu.make_async_copy(
                returned.at[b], out.at[:, i, pl.ds(q * CHUNK + t * LANE, LANE)], out_sem.at[b]
            )

        for q in range(chunks):
            pltpu.make_async_copy(gathered.at[q], gathered.at[q], back_recv.at[q]).wait()
            for i in range(rows):
                for t in range(CHUNK // LANE):
                    write(q, i, t).start()

        sent = gathered.at[0, pl.ds(0, (comp_count - 1) * comp_local)]
        for q, (low, size) in enumerate(parts):
            pltpu.make_async_copy(sent, sent, there_send.at[q]).wait()
            pltpu.make_async_copy(sent, sent, back_send.at[q]).wait()
            part = halo.at[own(low, size)]
            pltpu.make_async_copy(part, part, halo_send.at[q]).wait()
        for q in range(chunks):
            for i in range(rows):
                for t in range(CHUNK // LANE):
                    write(q, i, t).wait()

    return kernel


def per_device(energy, sea_mask, depth_class, group_speed, wind_input, whitecap, pair_in, pair_out):
    comp_count = lax.axis_size("comp")
    lat_count = lax.axis_size("lat")
    comp_local, rows, lon = energy.shape
    total = comp_local * comp_count
    chunks = lon // CHUNK
    lat_place = lax.axis_index("lat")
    comp_place = lax.axis_index("comp")
    comp_ids = comp_place * comp_local + jnp.arange(comp_local)
    angles = 2.0 * math.pi * ((comp_ids % NDIR).astype(F32) + 0.5) / NDIR
    speed_table = lax.dynamic_slice_in_dim(
        jnp.repeat(group_speed, NDIR, axis=0), comp_place * comp_local, comp_local, 0
    )
    table = jnp.concatenate(
        [speed_table, jnp.cos(angles)[:, None], jnp.sin(angles)[:, None]], axis=1
    )
    rates = jnp.stack([wind_input, whitecap], axis=1)

    def band(x):
        x = jnp.pad(x, ((SUB, SUB), (LANE, LANE)))
        return lax.dynamic_slice_in_dim(x, lat_place * rows, rows + 2 * SUB, 0)

    sea = band(sea_mask).astype(F32)
    classes = band(depth_class)
    blocks = chunks * comp_count
    anywhere = pl.BlockSpec(memory_space=pl.ANY)
    near = pl.BlockSpec(memory_space=pltpu.VMEM)
    dma = pltpu.SemaphoreType.DMA
    return pl.pallas_call(
        make_kernel(comp_count, lat_count, comp_local, rows, lon),
        out_shape=jax.ShapeDtypeStruct(energy.shape, F32),
        in_specs=[anywhere] * 3 + [near] * 4,
        out_specs=anywhere,
        scratch_shapes=[
            pltpu.VMEM((lon // LANE + 2, rows, comp_local, LANE), F32),
            pltpu.VMEM((lon // LANE + 2, 2, comp_local, LANE), F32),
            pltpu.VMEM((blocks, comp_local, LANE), F32),
            pltpu.VMEM((chunks, total, LANE), F32),
            pltpu.VMEM((blocks, comp_local, LANE), F32),
            pltpu.VMEM((total, total), BF16),
            pltpu.VMEM((total, total), BF16),
            pltpu.VMEM((total, LANE), BF16),
            pltpu.VMEM((total, LANE), BF16),
            dma((chunks,)),
            dma((2,)),
            dma((chunks,)),
            dma((chunks,)),
            dma((chunks,)),
            dma((chunks,)),
            dma((chunks,)),
            dma((chunks,)),
            dma((blocks,)),
        ],
        compiler_params=pltpu.CompilerParams(
            collective_id=0, has_side_effects=True, vmem_limit_bytes=58 * 2**20
        ),
        cost_estimate=pl.CostEstimate(
            flops=4 * total * total * chunks * LANE, bytes_accessed=24 * 2**20, transcendentals=0
        ),
    )(energy, pair_in, pair_out, sea, classes, table, rates)


def solution(mesh):
    placed = (P("comp", "lat", None), P(), P(), P(), P(), P(), P(), P())
    return jax.shard_map(
        per_device, mesh=mesh, in_specs=placed, out_specs=P("comp", "lat", None), check_vma=False
    )
```

```python
import math

import jax
import numpy as np
import jax.numpy as jnp
from jax import lax
from jax.experimental import pallas as pl
from jax.experimental.pallas import tpu as pltpu
from jax.sharding import PartitionSpec as P

NDIR = 36
SUB = 2
MESH = pl.DeviceIdType.MESH
F32 = jnp.float32
BF16 = jnp.bfloat16

time_step = 0.5

LANE = 128
CHUNK = 256
RUN = 18
EARLY = 3
PAIR = 2


def sections(lon):
    tiles, step = lon // LANE, CHUNK // LANE
    ends = [0] + [min(step * (q + 1) + 1, tiles) for q in range(lon // CHUNK)]
    return [(low, high - low) for low, high in zip(ends, ends[1:])]


def make_kernel(comp_count, lat_count, comp_local, rows, lon):
    chunks = lon // CHUNK
    total = comp_count * comp_local
    parts = sections(lon)
    tiles = lon // LANE
    spread = CHUNK // LANE + 1
    window = spread * LANE
    groups = comp_local // 8
    runs = comp_local // RUN
    rest = comp_local - runs * RUN
    quarter = runs // 4
    tail_groups = [*range(groups // PAIR * PAIR * 8, comp_local - 7, 8), comp_local - 8]
    row_tiles = [(0, 448), (448, 448), (896, 448), (1344, total - 1344)]

    def kernel(
        energy,
        pair_in,
        pair_out,
        sea_mask,
        depth_class,
        group_speed,
        wind_input,
        whitecap,
        out,
        cells,
        halo,
        early,
        advected,
        gathered,
        returned,
        map_in,
        map_out,
        half,
        terms,
        mask_rows,
        class_rows,
        sea,
        classes,
        rates_rows,
        rates,
        trig,
        load_sem,
        fact_sem,
        map_sem,
        halo_send,
        halo_recv,
        there_send,
        there_recv,
        back_send,
        back_recv,
        out_sem,
    ):
        c = lax.axis_index("comp")
        l = lax.axis_index("lat")
        odd = lax.rem(c, 2)

        def own(low, size):
            return pl.ds(low + 1, size)

        def load_cells(q):
            low, size = parts[q]
            for tile in range(low, low + size):
                for r in range(rows):
                    pltpu.make_async_copy(
                        energy.at[:, r, pl.ds(tile * LANE, LANE)],
                        cells.at[tile + 1, r],
                        load_sem.at[q],
                    ).start()

        def wait_cells(q):
            low, size = parts[q]
            part = cells.at[own(low, size)]
            pltpu.make_async_copy(part, part, load_sem.at[q]).wait()

        lat_rows = lat_count * rows
        fact_low = jnp.clip((l * rows - SUB + 8) // 8 - 1, 0, lat_rows // 8 - 2) * 8
        fact_rows = pl.ds(pl.multiple_of(fact_low, 8), 16)
        fact_copies = [
            pltpu.make_async_copy(sea_mask.at[fact_rows], mask_rows, fact_sem.at[0]),
            pltpu.make_async_copy(depth_class.at[fact_rows], class_rows, fact_sem.at[1]),
        ]
        for copy in fact_copies:
            copy.start()
        for q in range(chunks):
            load_cells(q)

        barrier = pltpu.get_barrier_semaphore()
        north = lax.rem(l + 1, lat_count)
        south = lax.rem(l + lat_count - 1, lat_count)
        for d in range(1, comp_count):
            pl.semaphore_signal(
                barrier, inc=1, device_id=(lax.rem(c + d, comp_count), l), device_id_type=MESH
            )
        for other in (north, south):
            pl.semaphore_signal(barrier, inc=1, device_id=(c, other), device_id_type=MESH)

        angles = 2.0 * math.pi * (np.arange(trig.shape[1]) % NDIR + 0.5) / NDIR
        for i, values in enumerate((np.cos(angles), np.sin(angles))):
            for j, value in enumerate(values):
                trig[i, j : j + 1, :] = jnp.full((1, LANE), value, F32)

        lane = lax.broadcasted_iota(jnp.int32, (8, LANE), 1)

        def edge(before, after):
            return jnp.where(lane < LANE // 2, after, before)

        for copy in fact_copies:
            copy.wait()
        for i in range(rows + 2 * SUB):
            row = l * rows + i - SUB
            inside = jnp.logical_and(row >= 0, row < lat_rows).astype(jnp.int32)
            at = pl.ds(jnp.clip(row, 0, lat_rows - 1) - fact_low, 1)
            for ref, values in (
                (sea, (mask_rows[at, :] * inside).astype(F32)),
                (classes, class_rows[at, :]),
            ):
                blank = jnp.zeros((8, LANE), values.dtype)
                wide = [
                    jnp.broadcast_to(values[:, k * LANE : (k + 1) * LANE], (8, LANE))
                    for k in range(tiles)
                ]
                wide = [blank] + wide + [blank]
                for q in range(chunks):
                    first = q * (CHUNK // LANE)
                    for t in range(spread - 1):
                        ref[i, q * spread + t] = wide[first + 1 + t]
                    ref[i, q * spread + spread - 1] = edge(wide[first], wide[first + spread])

        def send_halo(start, count, up, q):
            low, size = parts[q]
            for near in range(2):
                for is_up in (True, False):

                    @pl.when(up if is_up else jnp.logical_not(up))
                    def _():
                        pltpu.make_async_remote_copy(
                            src_ref=cells.at[
                                own(low, size),
                                rows - 1 - near if is_up else near,
                                pl.ds(start, count),
                            ],
                            dst_ref=halo.at[own(low, size), near, pl.ds(start, count)],
                            send_sem=halo_send.at[q],
                            recv_sem=halo_recv.at[q],
                            device_id=(c, north if is_up else south),
                            device_id_type=MESH,
                        ).start()

        def run_of(m):
            return m * RUN + odd * rest, lax.rem((c + odd) // 2 + m, 2) == 0

        rest_run = ((1 - odd) * runs * RUN, lax.rem(c, 4) < 2)

        def send_halos(q):
            if q >= EARLY:
                wait_cells(q)

            @pl.loop(0, runs)
            def _(m):
                start, up = run_of(m)
                send_halo(start, RUN, up, q)

            send_halo(rest_run[0], rest, rest_run[1], q)

        def meet():
            pl.semaphore_wait(barrier, comp_count + 1)

        def after_first():
            for q in range(EARLY):
                send_halos(q)

        def advect_group(q, start, wanted, put):
            here = pl.ds(start, 8)
            tile = q * (CHUNK // LANE)
            ident = c * comp_local + start
            first_tile = q * spread
            sublane = lax.broadcasted_iota(jnp.int32, (8, LANE), 0)
            low_freq = ident // NDIR
            high_freq = (ident + 7) // NDIR
            later = sublane + lax.rem(ident, NDIR) >= NDIR

            def wide(v):
                return jnp.concatenate([v] * spread, axis=1)

            angle = pl.ds(lax.rem(ident, NDIR), 8)
            cosine, sine = wide(trig[0, angle, :]), wide(trig[1, angle, :])
            up = sine > 0.0
            eastward = cosine > 0.0
            speeds = [
                wide(jnp.where(later, group_speed[j, high_freq], group_speed[j, low_freq]))
                for j in range(8)
            ]

            def strip(ref, i):
                parts = [ref[tile + t, i, here, :] for t in range(spread + 1)]
                return jnp.concatenate(parts[1:-1] + [edge(parts[0], parts[-1])], axis=1)

            def fact(ref, i):
                return jnp.concatenate([ref[i, first_tile + t] for t in range(spread)], axis=1)

            def facing(ref, i):
                return jnp.where(up, fact(ref, i + SUB), fact(ref, SUB + rows - 1 - i))

            def upstream(i):
                wet = facing(sea, i)
                if i < 0:
                    value = strip(halo, -1 - i)
                else:
                    value = jnp.where(up, strip(cells, i), strip(cells, rows - 1 - i))
                return jnp.where(wet > 0.0, value, 0.0), wet

            def rates_of(i):
                kinds = facing(classes, i)
                speed = speeds[0]
                for level in range(1, 8):
                    speed = jnp.where(kinds == level, speeds[level], speed)
                return jnp.abs(speed * cosine), jnp.abs(speed * sine)

            def beside(v):
                return jnp.where(eastward, pltpu.roll(v, 1, 1), pltpu.roll(v, window - 1, 1))

            def moved(v, across, zonal, meridional, wet):
                return (v - zonal * (v - beside(v)) - meridional * (v - across)) * wet

            behind, _ = upstream(wanted[0] - 2)
            earlier = None
            for i in range(wanted[0] - 1, wanted[-1] + 1):
                value, wet = upstream(i)
                speed = rates_of(i)
                first = moved(value, behind, *speed, wet)
                behind = value
                if i >= wanted[0]:
                    second = moved(first, earlier, *speed, wet)
                    for t in range(CHUNK // LANE):
                        put(i, t, here, second[:, LANE * t : LANE * (t + 1)], up[:, :LANE])
                earlier = first

        def wait_part(q):
            for k, (low, size) in enumerate(parts):

                @pl.when(q == k)
                def _():
                    part = halo.at[own(low, size)]
                    pltpu.make_async_copy(part, part, halo_recv.at[k]).wait()

        def send_run(ref, base, q, start, count, up, ahead):
            for j in range(comp_count // 2):
                home = jnp.where(up == ahead, comp_count // 2 + j, j)
                source = ref.at[base + home, pl.ds(start, count)]
                place = gathered.at[q, pl.ds(c * comp_local + start, count)]

                @pl.when(home == c)
                def _():
                    pltpu.make_async_copy(source, place, there_recv.at[q]).start()

                @pl.when(home != c)
                def _():
                    pltpu.make_async_remote_copy(
                        src_ref=source,
                        dst_ref=place,
                        send_sem=there_send.at[q],
                        recv_sem=there_recv.at[q],
                        device_id=(home, l),
                        device_id_type=MESH,
                    ).start()

        def by_halves(ref, q, wanted, ahead, before_send=None):
            base = q * comp_count

            def put(i, t, here, values, up):
                ref[base + i * 2 + t, here, :] = values
                ref[base + (rows - 1 - i) * 2 + t, here, :] = values

            done = 0
            for k in range(4):
                need = comp_local if k == 3 else (k + 1) * quarter * RUN + rest
                ready = min(-(-need // (8 * PAIR)), groups // PAIR)

                @pl.loop(done, ready)
                def _(g):
                    for h in range(PAIR):
                        advect_group(q, pl.multiple_of(g * (8 * PAIR) + h * 8, 8), wanted, put)

                done = ready
                if k == 3:
                    for start in tail_groups:
                        advect_group(q, start, wanted, put)
                if before_send is not None and k == 0:
                    before_send()

                @pl.loop(k * quarter, (k + 1) * quarter)
                def _(m):
                    start, up = run_of(m)
                    send_run(ref, base, q, start, RUN, up, ahead)

                if before_send is not None and k == 0:
                    after_first()

            send_run(ref, base, q, rest_run[0], rest, rest_run[1], ahead)

        for q in range(EARLY):
            wait_cells(q)
        for q in range(EARLY):
            by_halves(early, q, (2, 3), True, meet if q == 0 else None)
        for q in range(EARLY, chunks):
            send_halos(q)
        pltpu.make_async_copy(pair_in, map_in, map_sem.at[0]).start()
        pltpu.make_async_copy(pair_out, map_out, map_sem.at[1]).start()
        for q in range(EARLY):
            wait_part(q)
            by_halves(advected, q, (0, 1), False)

        @pl.loop(EARLY, chunks)
        def _(q):
            wait_part(q)
            held = {}

            def put(i, t, here, values, up):
                held[i, t] = values
                if i >= rows // 2:
                    mirror = held[rows - 1 - i, t]
                    base = q * comp_count + t
                    advected[base + i * 2, here, :] = jnp.where(up, values, mirror)
                    advected[base + (rows - 1 - i) * 2, here, :] = jnp.where(up, mirror, values)

            @pl.loop(0, groups // PAIR)
            def _(g):
                for h in range(PAIR):
                    advect_group(q, pl.multiple_of(g * (8 * PAIR) + h * 8, 8), (0, 1, 2, 3), put)

            for start in tail_groups:
                advect_group(q, start, (0, 1, 2, 3), put)

            place = gathered.at[q, pl.ds(c * comp_local, comp_local)]
            pltpu.make_async_copy(advected.at[q * comp_count + c], place, there_recv.at[q]).start()

            @pl.loop(1, comp_count)
            def _(d):
                home = lax.rem(c + d, comp_count)
                pltpu.make_async_remote_copy(
                    src_ref=advected.at[q * comp_count + home],
                    dst_ref=place,
                    send_sem=there_send.at[q],
                    recv_sem=there_recv.at[q],
                    device_id=(home, l),
                    device_id_type=MESH,
                ).start()

        for i, ref in enumerate((wind_input, whitecap)):
            for low in range(0, total, LANE):
                size = min(LANE, total - low)
                rates_rows[i : i + 1, low : low + size] = ref[pl.ds(low, size)].reshape(1, size)
        rates[...] = rates_rows[...].T

        pltpu.make_async_copy(pair_in, map_in, map_sem.at[0]).wait()
        pltpu.make_async_copy(pair_out, map_out, map_sem.at[1]).wait()

        @pl.loop(0, chunks)
        def _(q):
            pltpu.make_async_copy(gathered.at[q], gathered.at[q], there_recv.at[q]).wait()
            spectra = gathered[q]
            half[...] = spectra.astype(BF16)
            mean_energy = jnp.sum(spectra, axis=0, keepdims=True) * (1.0 / total)
            for low, size in row_tiles:
                projected = jnp.dot(
                    map_in[low : low + size, :], half[...], preferred_element_type=F32
                )
                terms[low : low + size, :] = (
                    projected * gathered[q, low : low + size, :]
                ).astype(BF16)
            for low, size in row_tiles:
                transfer = jnp.dot(
                    map_out[low : low + size, :], terms[...], preferred_element_type=F32
                )
                now = gathered[q, low : low + size, :]
                wind = rates[low : low + size, 0:1]
                white = rates[low : low + size, 1:2]
                gathered[q, low : low + size, :] = now + time_step * (
                    wind * now - white * mean_energy * now + transfer
                )

            place = returned.at[q * comp_count + c]
            pltpu.make_async_copy(
                gathered.at[q, pl.ds(c * comp_local, comp_local)], place, back_recv.at[q]
            ).start()

            @pl.loop(1, comp_count)
            def _(d):
                origin = lax.rem(c + d, comp_count)
                pltpu.make_async_remote_copy(
                    src_ref=gathered.at[q, pl.ds(origin * comp_local, comp_local)],
                    dst_ref=place,
                    send_sem=back_send.at[q],
                    recv_sem=back_recv.at[q],
                    device_id=(origin, l),
                    device_id_type=MESH,
                ).start()

        def write(q, i, t):
            b = q * comp_count + i * 2 + t
            return pltpu.make_async_copy(
                returned.at[b], out.at[:, i, pl.ds(q * CHUNK + t * LANE, LANE)], out_sem.at[b]
            )

        for q in range(chunks):
            pltpu.make_async_copy(gathered.at[q], gathered.at[q], back_recv.at[q]).wait()
            for i in range(rows):
                for t in range(CHUNK // LANE):
                    write(q, i, t).start()

        sent = gathered.at[0, pl.ds(0, (comp_count - 1) * comp_local)]
        for q, (low, size) in enumerate(parts):
            pltpu.make_async_copy(sent, sent, there_send.at[q]).wait()
            pltpu.make_async_copy(sent, sent, back_send.at[q]).wait()
            part = halo.at[own(low, size)]
            pltpu.make_async_copy(part, part, halo_send.at[q]).wait()
        for q in range(chunks):
            for i in range(rows):
                for t in range(CHUNK // LANE):
                    write(q, i, t).wait()

    return kernel


def per_device(energy, sea_mask, depth_class, group_speed, wind_input, whitecap, pair_in, pair_out):
    comp_count = lax.axis_size("comp")
    lat_count = lax.axis_size("lat")
    comp_local, rows, lon = energy.shape
    total = comp_local * comp_count
    chunks = lon // CHUNK
    blocks = chunks * comp_count
    anywhere = pl.BlockSpec(memory_space=pl.ANY)
    near = pl.BlockSpec(memory_space=pltpu.VMEM)
    dma = pltpu.SemaphoreType.DMA
    return pl.pallas_call(
        make_kernel(comp_count, lat_count, comp_local, rows, lon),
        out_shape=jax.ShapeDtypeStruct(energy.shape, F32),
        in_specs=[anywhere] * 5 + [pl.BlockSpec(memory_space=pltpu.SMEM), near, near],
        out_specs=anywhere,
        scratch_shapes=[
            pltpu.VMEM((lon // LANE + 2, rows, comp_local, LANE), F32),
            pltpu.VMEM((lon // LANE + 2, 2, comp_local, LANE), F32),
            pltpu.VMEM((EARLY * comp_count, comp_local, LANE), F32),
            pltpu.VMEM((blocks, comp_local, LANE), F32),
            pltpu.VMEM((chunks, total, LANE), F32),
            pltpu.VMEM((blocks, comp_local, LANE), F32),
            pltpu.VMEM((total, total), BF16),
            pltpu.VMEM((total, total), BF16),
            pltpu.VMEM((total, LANE), BF16),
            pltpu.VMEM((total, LANE), BF16),
            pltpu.VMEM((16, lon), jnp.int32),
            pltpu.VMEM((16, lon), jnp.int32),
            pltpu.VMEM((rows + 2 * SUB, chunks * (CHUNK // LANE + 1), 8, LANE), F32),
            pltpu.VMEM((rows + 2 * SUB, chunks * (CHUNK // LANE + 1), 8, LANE), jnp.int32),
            pltpu.VMEM((8, total), F32),
            pltpu.VMEM((total, 8), F32),
            pltpu.VMEM((2, NDIR + 8, LANE), F32),
            dma((chunks,)),
            dma((2,)),
            dma((2,)),
            dma((chunks,)),
            dma((chunks,)),
            dma((chunks,)),
            dma((chunks,)),
            dma((chunks,)),
            dma((chunks,)),
            dma((blocks,)),
        ],
        compiler_params=pltpu.CompilerParams(
            collective_id=0, has_side_effects=True, vmem_limit_bytes=58 * 2**20
        ),
        cost_estimate=pl.CostEstimate(
            flops=4 * total * total * chunks * LANE, bytes_accessed=24 * 2**20, transcendentals=0
        ),
    )(energy, pair_in, pair_out, sea_mask, depth_class, group_speed.T, wind_input, whitecap)


def solution(mesh):
    placed = (P("comp", "lat", None), P(), P(), P(), P(), P(), P(), P())
    return jax.shard_map(
        per_device, mesh=mesh, in_specs=placed, out_specs=P("comp", "lat", None), check_vma=False
    )
```

```python
import math

import jax
import numpy as np
import jax.numpy as jnp
from jax import lax
from jax.experimental import pallas as pl
from jax.experimental.pallas import tpu as pltpu
from jax.sharding import PartitionSpec as P

NDIR = 36
SUB = 2
MESH = pl.DeviceIdType.MESH
F32 = jnp.float32
BF16 = jnp.bfloat16

time_step = 0.5

LANE = 128
CHUNK = 256
RUN = 18
EARLY = 3
PAIR = 2


def sections(lon):
    tiles, step = lon // LANE, CHUNK // LANE
    ends = [0] + [min(step * (q + 1) + 1, tiles) for q in range(lon // CHUNK)]
    return [(low, high - low) for low, high in zip(ends, ends[1:])]


def make_kernel(comp_count, lat_count, comp_local, rows, lon):
    chunks = lon // CHUNK
    total = comp_count * comp_local
    parts = sections(lon)
    tiles = lon // LANE
    spread = CHUNK // LANE + 1
    window = spread * LANE
    groups = comp_local // 8
    runs = comp_local // RUN
    rest = comp_local - runs * RUN
    quarter = runs // 4
    tail_groups = [*range(groups // PAIR * PAIR * 8, comp_local - 7, 8), comp_local - 8]
    row_tiles = [(0, 448), (448, 448), (896, 448), (1344, total - 1344)]

    def kernel(
        energy,
        pair_in,
        pair_out,
        sea_mask,
        depth_class,
        group_speed,
        wind_input,
        whitecap,
        returned,
        cells,
        halo,
        early,
        advected,
        gathered,
        map_in,
        map_out,
        half,
        terms,
        mask_rows,
        class_rows,
        sea,
        classes,
        rates_rows,
        rates,
        trig,
        load_sem,
        fact_sem,
        map_sem,
        halo_send,
        halo_recv,
        there_send,
        there_recv,
        back_send,
        back_recv,
    ):
        c = lax.axis_index("comp")
        l = lax.axis_index("lat")
        odd = lax.rem(c, 2)

        def own(low, size):
            return pl.ds(low + 1, size)

        def load_cells(q):
            low, size = parts[q]
            for tile in range(low, low + size):
                for r in range(rows):
                    pltpu.make_async_copy(
                        energy.at[:, r, pl.ds(tile * LANE, LANE)],
                        cells.at[tile + 1, r],
                        load_sem.at[q],
                    ).start()

        def wait_cells(q):
            low, size = parts[q]
            part = cells.at[own(low, size)]
            pltpu.make_async_copy(part, part, load_sem.at[q]).wait()

        lat_rows = lat_count * rows
        fact_low = jnp.clip((l * rows - SUB + 8) // 8 - 1, 0, lat_rows // 8 - 2) * 8
        fact_rows = pl.ds(pl.multiple_of(fact_low, 8), 16)
        fact_copies = [
            pltpu.make_async_copy(sea_mask.at[fact_rows], mask_rows, fact_sem.at[0]),
            pltpu.make_async_copy(depth_class.at[fact_rows], class_rows, fact_sem.at[1]),
        ]
        for copy in fact_copies:
            copy.start()
        for q in range(EARLY - 1):
            load_cells(q)

        barrier = pltpu.get_barrier_semaphore()
        north = lax.rem(l + 1, lat_count)
        south = lax.rem(l + lat_count - 1, lat_count)
        for d in range(1, comp_count):
            pl.semaphore_signal(
                barrier, inc=1, device_id=(lax.rem(c + d, comp_count), l), device_id_type=MESH
            )
        for other in (north, south):
            pl.semaphore_signal(barrier, inc=1, device_id=(c, other), device_id_type=MESH)

        angles = 2.0 * math.pi * (np.arange(trig.shape[1]) % NDIR + 0.5) / NDIR
        for i, values in enumerate((np.cos(angles), np.sin(angles))):
            for j, value in enumerate(values):
                trig[i, j : j + 1, :] = jnp.full((1, LANE), value, F32)

        lane = lax.broadcasted_iota(jnp.int32, (8, LANE), 1)

        def edge(before, after):
            return jnp.where(lane < LANE // 2, after, before)

        for copy in fact_copies:
            copy.wait()
        for i in range(rows + 2 * SUB):
            row = l * rows + i - SUB
            inside = jnp.logical_and(row >= 0, row < lat_rows).astype(jnp.int32)
            at = pl.ds(jnp.clip(row, 0, lat_rows - 1) - fact_low, 1)
            for ref, values in (
                (sea, (mask_rows[at, :] * inside).astype(F32)),
                (classes, class_rows[at, :]),
            ):
                blank = jnp.zeros((8, LANE), values.dtype)
                wide = [
                    jnp.broadcast_to(values[:, k * LANE : (k + 1) * LANE], (8, LANE))
                    for k in range(tiles)
                ]
                wide = [blank] + wide + [blank]
                for q in range(chunks):
                    first = q * (CHUNK // LANE)
                    for t in range(spread - 1):
                        ref[i, q * spread + t] = wide[first + 1 + t]
                    ref[i, q * spread + spread - 1] = edge(wide[first], wide[first + spread])
        for q in range(EARLY - 1, chunks):
            load_cells(q)

        def send_halo(start, count, up, q):
            low, size = parts[q]
            for near in range(2):
                for is_up in (True, False):

                    @pl.when(up if is_up else jnp.logical_not(up))
                    def _():
                        pltpu.make_async_remote_copy(
                            src_ref=cells.at[
                                own(low, size),
                                rows - 1 - near if is_up else near,
                                pl.ds(start, count),
                            ],
                            dst_ref=halo.at[own(low, size), near, pl.ds(start, count)],
                            send_sem=halo_send.at[q],
                            recv_sem=halo_recv.at[q],
                            device_id=(c, north if is_up else south),
                            device_id_type=MESH,
                        ).start()

        def run_of(m):
            return m * RUN + odd * rest, lax.rem((c + odd) // 2 + m, 2) == 0

        rest_run = ((1 - odd) * runs * RUN, lax.rem(c, 4) < 2)

        def send_halos(q):
            if q > 0:
                wait_cells(q)

            @pl.loop(0, runs)
            def _(m):
                start, up = run_of(m)
                send_halo(start, RUN, up, q)

            send_halo(rest_run[0], rest, rest_run[1], q)

        def advect_group(q, start, wanted, put):
            here = pl.ds(start, 8)
            tile = q * (CHUNK // LANE)
            ident = c * comp_local + start
            first_tile = q * spread
            sublane = lax.broadcasted_iota(jnp.int32, (8, LANE), 0)
            low_freq = ident // NDIR
            high_freq = (ident + 7) // NDIR
            later = sublane + lax.rem(ident, NDIR) >= NDIR

            def wide(v):
                return jnp.concatenate([v] * spread, axis=1)

            angle = pl.ds(lax.rem(ident, NDIR), 8)
            cosine, sine = wide(trig[0, angle, :]), wide(trig[1, angle, :])
            up = sine > 0.0
            eastward = cosine > 0.0
            speeds = [
                wide(jnp.where(later, group_speed[j, high_freq], group_speed[j, low_freq]))
                for j in range(8)
            ]

            def strip(ref, i):
                parts = [ref[tile + t, i, here, :] for t in range(spread + 1)]
                return jnp.concatenate(parts[1:-1] + [edge(parts[0], parts[-1])], axis=1)

            def fact(ref, i):
                return jnp.concatenate([ref[i, first_tile + t] for t in range(spread)], axis=1)

            def facing(ref, i):
                return jnp.where(up, fact(ref, i + SUB), fact(ref, SUB + rows - 1 - i))

            def upstream(i):
                wet = facing(sea, i)
                if i < 0:
                    value = strip(halo, -1 - i)
                else:
                    value = jnp.where(up, strip(cells, i), strip(cells, rows - 1 - i))
                return jnp.where(wet > 0.0, value, 0.0), wet

            def rates_of(i):
                kinds = facing(classes, i)
                speed = speeds[0]
                for level in range(1, 8):
                    speed = jnp.where(kinds == level, speeds[level], speed)
                return jnp.abs(speed * cosine), jnp.abs(speed * sine)

            def beside(v):
                return jnp.where(eastward, pltpu.roll(v, 1, 1), pltpu.roll(v, window - 1, 1))

            def moved(v, across, zonal, meridional, wet):
                return (v - zonal * (v - beside(v)) - meridional * (v - across)) * wet

            behind, _ = upstream(wanted[0] - 2)
            earlier = None
            for i in range(wanted[0] - 1, wanted[-1] + 1):
                value, wet = upstream(i)
                speed = rates_of(i)
                first = moved(value, behind, *speed, wet)
                behind = value
                if i >= wanted[0]:
                    second = moved(first, earlier, *speed, wet)
                    for t in range(CHUNK // LANE):
                        put(i, t, here, second[:, LANE * t : LANE * (t + 1)], up[:, :LANE])
                earlier = first

        def wait_part(q):
            for k, (low, size) in enumerate(parts):

                @pl.when(q == k)
                def _():
                    part = halo.at[own(low, size)]
                    pltpu.make_async_copy(part, part, halo_recv.at[k]).wait()

        def send_run(ref, base, q, start, count, up, ahead):
            for j in range(comp_count // 2):
                home = jnp.where(up == ahead, comp_count // 2 + j, j)
                source = ref.at[base + home, pl.ds(start, count)]
                place = gathered.at[q, pl.ds(c * comp_local + start, count)]

                @pl.when(home == c)
                def _():
                    pltpu.make_async_copy(source, place, there_recv.at[q]).start()

                @pl.when(home != c)
                def _():
                    pltpu.make_async_remote_copy(
                        src_ref=source,
                        dst_ref=place,
                        send_sem=there_send.at[q],
                        recv_sem=there_recv.at[q],
                        device_id=(home, l),
                        device_id_type=MESH,
                    ).start()

        def by_halves(ref, q, wanted, ahead, opening=False):
            base = q * comp_count

            def put(i, t, here, values, up):
                ref[base + i * 2 + t, here, :] = values
                ref[base + (rows - 1 - i) * 2 + t, here, :] = values

            def send_quarter(k):
                @pl.loop(k * quarter, (k + 1) * quarter)
                def _(m):
                    start, up = run_of(m)
                    send_run(ref, base, q, start, RUN, up, ahead)

            done = 0
            for k in range(4):
                need = comp_local if k == 3 else (k + 1) * quarter * RUN + rest
                ready = min(-(-need // (8 * PAIR)), groups // PAIR)

                @pl.loop(done, ready)
                def _(g):
                    for h in range(PAIR):
                        advect_group(q, pl.multiple_of(g * (8 * PAIR) + h * 8, 8), wanted, put)

                done = ready
                if k == 3:
                    for start in tail_groups:
                        advect_group(q, start, wanted, put)
                if not opening or k > 1:
                    send_quarter(k)
                elif k == 1:
                    pl.semaphore_wait(barrier, comp_count + 1)
                    send_quarter(0)
                    send_quarter(1)
                    for part in range(EARLY):
                        send_halos(part)

            send_run(ref, base, q, rest_run[0], rest, rest_run[1], ahead)

        wait_cells(0)
        for q in range(EARLY):
            by_halves(early, q, (2, 3), True, opening=q == 0)
        for q in range(EARLY, chunks):
            send_halos(q)
        pltpu.make_async_copy(pair_in, map_in, map_sem.at[0]).start()
        pltpu.make_async_copy(pair_out, map_out, map_sem.at[1]).start()
        for q in range(EARLY):
            wait_part(q)
            by_halves(advected, q, (0, 1), False)

        @pl.loop(EARLY, chunks)
        def _(q):
            wait_part(q)
            held = {}

            def put(i, t, here, values, up):
                held[i, t] = values
                if i >= rows // 2:
                    mirror = held[rows - 1 - i, t]
                    base = q * comp_count + t
                    advected[base + i * 2, here, :] = jnp.where(up, values, mirror)
                    advected[base + (rows - 1 - i) * 2, here, :] = jnp.where(up, mirror, values)

            @pl.loop(0, groups // PAIR)
            def _(g):
                for h in range(PAIR):
                    advect_group(q, pl.multiple_of(g * (8 * PAIR) + h * 8, 8), (0, 1, 2, 3), put)

            for start in tail_groups:
                advect_group(q, start, (0, 1, 2, 3), put)

            place = gathered.at[q, pl.ds(c * comp_local, comp_local)]
            pltpu.make_async_copy(advected.at[q * comp_count + c], place, there_recv.at[q]).start()

            @pl.loop(1, comp_count)
            def _(d):
                home = lax.rem(c + d, comp_count)
                pltpu.make_async_remote_copy(
                    src_ref=advected.at[q * comp_count + home],
                    dst_ref=place,
                    send_sem=there_send.at[q],
                    recv_sem=there_recv.at[q],
                    device_id=(home, l),
                    device_id_type=MESH,
                ).start()

        for i, ref in enumerate((wind_input, whitecap)):
            for low in range(0, total, LANE):
                size = min(LANE, total - low)
                rates_rows[i : i + 1, low : low + size] = ref[pl.ds(low, size)].reshape(1, size)
        rates[...] = rates_rows[...].T

        pltpu.make_async_copy(pair_in, map_in, map_sem.at[0]).wait()
        pltpu.make_async_copy(pair_out, map_out, map_sem.at[1]).wait()

        @pl.loop(0, chunks)
        def _(q):
            pltpu.make_async_copy(gathered.at[q], gathered.at[q], there_recv.at[q]).wait()
            spectra = gathered[q]
            half[...] = spectra.astype(BF16)
            mean_energy = jnp.sum(spectra, axis=0, keepdims=True) * (1.0 / total)
            for low, size in row_tiles:
                projected = jnp.dot(
                    map_in[low : low + size, :], half[...], preferred_element_type=F32
                )
                terms[low : low + size, :] = (
                    projected * gathered[q, low : low + size, :]
                ).astype(BF16)
            for low, size in row_tiles:
                transfer = jnp.dot(
                    map_out[low : low + size, :], terms[...], preferred_element_type=F32
                )
                now = gathered[q, low : low + size, :]
                wind = rates[low : low + size, 0:1]
                white = rates[low : low + size, 1:2]
                gathered[q, low : low + size, :] = now + time_step * (
                    wind * now - white * mean_energy * now + transfer
                )

            place = returned.at[q * comp_count + c]
            pltpu.make_async_copy(
                gathered.at[q, pl.ds(c * comp_local, comp_local)], place, back_recv.at[q]
            ).start()

            @pl.loop(1, comp_count)
            def _(d):
                origin = lax.rem(c + d, comp_count)
                pltpu.make_async_remote_copy(
                    src_ref=gathered.at[q, pl.ds(origin * comp_local, comp_local)],
                    dst_ref=place,
                    send_sem=back_send.at[q],
                    recv_sem=back_recv.at[q],
                    device_id=(origin, l),
                    device_id_type=MESH,
                ).start()

        for q in range(chunks):
            pltpu.make_async_copy(gathered.at[q], gathered.at[q], back_recv.at[q]).wait()

        sent = gathered.at[0, pl.ds(0, (comp_count - 1) * comp_local)]
        for q, (low, size) in enumerate(parts):
            pltpu.make_async_copy(sent, sent, there_send.at[q]).wait()
            pltpu.make_async_copy(sent, sent, back_send.at[q]).wait()
            part = halo.at[own(low, size)]
            pltpu.make_async_copy(part, part, halo_send.at[q]).wait()

    return kernel


def write_kernel(comp_count, rows, blocks):
    def kernel(returned, out, sem):
        copies = []
        for b in range(blocks):
            q, place = divmod(b, comp_count)
            i, t = divmod(place, CHUNK // LANE)
            lanes = pl.ds(q * CHUNK + t * LANE, LANE)
            copies.append(
                pltpu.make_async_copy(returned.at[b], out.at[:, i, lanes], sem.at[b])
            )
        for copy in copies:
            copy.start()
        for copy in copies:
            copy.wait()

    return kernel


def per_device(energy, sea_mask, depth_class, group_speed, wind_input, whitecap, pair_in, pair_out):
    comp_count = lax.axis_size("comp")
    lat_count = lax.axis_size("lat")
    comp_local, rows, lon = energy.shape
    total = comp_local * comp_count
    chunks = lon // CHUNK
    blocks = chunks * comp_count
    anywhere = pl.BlockSpec(memory_space=pl.ANY)
    near = pl.BlockSpec(memory_space=pltpu.VMEM)
    dma = pltpu.SemaphoreType.DMA
    returned = pl.pallas_call(
        make_kernel(comp_count, lat_count, comp_local, rows, lon),
        out_shape=pltpu.VMEM((blocks, comp_local, LANE), F32),
        in_specs=[anywhere] * 5 + [pl.BlockSpec(memory_space=pltpu.SMEM), near, near],
        out_specs=near,
        scratch_shapes=[
            pltpu.VMEM((lon // LANE + 2, rows, comp_local, LANE), F32),
            pltpu.VMEM((lon // LANE + 2, 2, comp_local, LANE), F32),
            pltpu.VMEM((EARLY * comp_count, comp_local, LANE), F32),
            pltpu.VMEM((blocks, comp_local, LANE), F32),
            pltpu.VMEM((chunks, total, LANE), F32),
            pltpu.VMEM((total, total), BF16),
            pltpu.VMEM((total, total), BF16),
            pltpu.VMEM((total, LANE), BF16),
            pltpu.VMEM((total, LANE), BF16),
            pltpu.VMEM((16, lon), jnp.int32),
            pltpu.VMEM((16, lon), jnp.int32),
            pltpu.VMEM((rows + 2 * SUB, chunks * (CHUNK // LANE + 1), 8, LANE), F32),
            pltpu.VMEM((rows + 2 * SUB, chunks * (CHUNK // LANE + 1), 8, LANE), jnp.int32),
            pltpu.VMEM((8, total), F32),
            pltpu.VMEM((total, 8), F32),
            pltpu.VMEM((2, NDIR + 8, LANE), F32),
            dma((chunks,)),
            dma((2,)),
            dma((2,)),
            dma((chunks,)),
            dma((chunks,)),
            dma((chunks,)),
            dma((chunks,)),
            dma((chunks,)),
            dma((chunks,)),
        ],
        compiler_params=pltpu.CompilerParams(
            collective_id=0, has_side_effects=True, vmem_limit_bytes=50 * 2**20
        ),
        cost_estimate=pl.CostEstimate(
            flops=4 * total * total * chunks * LANE, bytes_accessed=24 * 2**20, transcendentals=0
        ),
    )(energy, pair_in, pair_out, sea_mask, depth_class, group_speed.T, wind_input, whitecap)
    return pl.pallas_call(
        write_kernel(comp_count, rows, blocks),
        out_shape=jax.ShapeDtypeStruct(energy.shape, F32),
        in_specs=[near],
        out_specs=anywhere,
        scratch_shapes=[dma((blocks,))],
        compiler_params=pltpu.CompilerParams(vmem_limit_bytes=8 * 2**20),
    )(returned)


def solution(mesh):
    placed = (P("comp", "lat", None), P(), P(), P(), P(), P(), P(), P())
    return jax.shard_map(
        per_device, mesh=mesh, in_specs=placed, out_specs=P("comp", "lat", None), check_vma=False
    )
```

```python
import math

import jax
import numpy as np
import jax.numpy as jnp
from jax import lax
from jax.experimental import pallas as pl
from jax.experimental.pallas import tpu as pltpu
from jax.sharding import PartitionSpec as P

NDIR = 36
SUB = 2
MESH = pl.DeviceIdType.MESH
F32 = jnp.float32
BF16 = jnp.bfloat16

time_step = 0.5

LANE = 128
CHUNK = 256
RUN = 18
EARLY = 4
PAIR = 2


def sections(lon):
    tiles, step = lon // LANE, CHUNK // LANE
    ends = [0] + [min(step * (q + 1) + 1, tiles) for q in range(lon // CHUNK)]
    return [(low, high - low) for low, high in zip(ends, ends[1:])]


def make_kernel(comp_count, lat_count, comp_local, rows, lon):
    chunks = lon // CHUNK
    total = comp_count * comp_local
    parts = sections(lon)
    tiles = lon // LANE
    spread = CHUNK // LANE + 1
    window = spread * LANE
    groups = comp_local // 8
    runs = comp_local // RUN
    rest = comp_local - runs * RUN
    quarter = runs // 4
    tail_groups = [*range(groups // PAIR * PAIR * 8, comp_local - 7, 8), comp_local - 8]
    row_tiles = [(0, 448), (448, 448), (896, 448), (1344, total - 1344)]

    def kernel(
        energy,
        pair_in,
        pair_out,
        sea_mask,
        depth_class,
        group_speed,
        wind_input,
        whitecap,
        returned,
        cells,
        halo,
        early,
        advected,
        gathered,
        map_in,
        map_out,
        half,
        terms,
        mask_rows,
        class_rows,
        sea,
        classes,
        rates_rows,
        rates,
        trig,
        load_sem,
        fact_sem,
        map_sem,
        halo_send,
        halo_recv,
        there_send,
        there_recv,
        back_send,
        back_recv,
    ):
        c = lax.axis_index("comp")
        l = lax.axis_index("lat")
        odd = lax.rem(c, 2)

        def own(low, size):
            return pl.ds(low + 1, size)

        def load_cells(q):
            low, size = parts[q]
            for tile in range(low, low + size):
                for r in range(rows):
                    pltpu.make_async_copy(
                        energy.at[:, r, pl.ds(tile * LANE, LANE)],
                        cells.at[tile + 1, r],
                        load_sem.at[q],
                    ).start()

        def wait_cells(q):
            low, size = parts[q]
            part = cells.at[own(low, size)]
            pltpu.make_async_copy(part, part, load_sem.at[q]).wait()

        lat_rows = lat_count * rows
        fact_low = jnp.clip((l * rows - SUB + 8) // 8 - 1, 0, lat_rows // 8 - 2) * 8
        fact_rows = pl.ds(pl.multiple_of(fact_low, 8), 16)
        fact_copies = [
            pltpu.make_async_copy(sea_mask.at[fact_rows], mask_rows, fact_sem.at[0]),
            pltpu.make_async_copy(depth_class.at[fact_rows], class_rows, fact_sem.at[1]),
        ]
        for copy in fact_copies:
            copy.start()
        load_cells(0)

        barrier = pltpu.get_barrier_semaphore()
        north = lax.rem(l + 1, lat_count)
        south = lax.rem(l + lat_count - 1, lat_count)
        for d in range(1, comp_count):
            pl.semaphore_signal(
                barrier, inc=1, device_id=(lax.rem(c + d, comp_count), l), device_id_type=MESH
            )
        for other in (north, south):
            pl.semaphore_signal(barrier, inc=1, device_id=(c, other), device_id_type=MESH)

        angles = 2.0 * math.pi * (np.arange(trig.shape[1]) % NDIR + 0.5) / NDIR
        for i, values in enumerate((np.cos(angles), np.sin(angles))):
            for j, value in enumerate(values):
                trig[i, j : j + 1, :] = jnp.full((1, LANE), value, F32)

        lane = lax.broadcasted_iota(jnp.int32, (8, LANE), 1)

        def edge(before, after):
            return jnp.where(lane < LANE // 2, after, before)

        for copy in fact_copies:
            copy.wait()
        for i in range(rows + 2 * SUB):
            row = l * rows + i - SUB
            inside = jnp.logical_and(row >= 0, row < lat_rows).astype(jnp.int32)
            at = pl.ds(jnp.clip(row, 0, lat_rows - 1) - fact_low, 1)
            for ref, values in (
                (sea, (mask_rows[at, :] * inside).astype(F32)),
                (classes, class_rows[at, :]),
            ):
                blank = jnp.zeros((8, LANE), values.dtype)
                wide = [
                    jnp.broadcast_to(values[:, k * LANE : (k + 1) * LANE], (8, LANE))
                    for k in range(tiles)
                ]
                wide = [blank] + wide + [blank]
                for q in range(chunks):
                    first = q * (CHUNK // LANE)
                    for t in range(spread - 1):
                        ref[i, q * spread + t] = wide[first + 1 + t]
                    ref[i, q * spread + spread - 1] = edge(wide[first], wide[first + spread])
        for q in range(1, chunks):
            load_cells(q)

        def send_halo(start, count, up, q):
            low, size = parts[q]
            for near in range(2):
                for is_up in (True, False):

                    @pl.when(up if is_up else jnp.logical_not(up))
                    def _():
                        pltpu.make_async_remote_copy(
                            src_ref=cells.at[
                                own(low, size),
                                rows - 1 - near if is_up else near,
                                pl.ds(start, count),
                            ],
                            dst_ref=halo.at[own(low, size), near, pl.ds(start, count)],
                            send_sem=halo_send.at[q],
                            recv_sem=halo_recv.at[q],
                            device_id=(c, north if is_up else south),
                            device_id_type=MESH,
                        ).start()

        def run_of(m):
            return m * RUN + odd * rest, lax.rem((c + odd) // 2 + m, 2) == 0

        rest_run = ((1 - odd) * runs * RUN, lax.rem(c, 4) < 2)

        def send_halos(q):
            if q > 0:
                wait_cells(q)

            @pl.loop(0, runs)
            def _(m):
                start, up = run_of(m)
                send_halo(start, RUN, up, q)

            send_halo(rest_run[0], rest, rest_run[1], q)

        def advect_group(q, start, wanted, put):
            here = pl.ds(start, 8)
            tile = q * (CHUNK // LANE)
            ident = c * comp_local + start
            first_tile = q * spread
            sublane = lax.broadcasted_iota(jnp.int32, (8, LANE), 0)
            low_freq = ident // NDIR
            high_freq = (ident + 7) // NDIR
            later = sublane + lax.rem(ident, NDIR) >= NDIR

            def wide(v):
                return jnp.concatenate([v] * spread, axis=1)

            angle = pl.ds(lax.rem(ident, NDIR), 8)
            cosine, sine = wide(trig[0, angle, :]), wide(trig[1, angle, :])
            up = sine > 0.0
            eastward = cosine > 0.0
            speeds = [
                wide(jnp.where(later, group_speed[j, high_freq], group_speed[j, low_freq]))
                for j in range(8)
            ]

            def strip(ref, i):
                parts = [ref[tile + t, i, here, :] for t in range(spread + 1)]
                return jnp.concatenate(parts[1:-1] + [edge(parts[0], parts[-1])], axis=1)

            def fact(ref, i):
                return jnp.concatenate([ref[i, first_tile + t] for t in range(spread)], axis=1)

            def facing(ref, i):
                return jnp.where(up, fact(ref, i + SUB), fact(ref, SUB + rows - 1 - i))

            def upstream(i):
                wet = facing(sea, i)
                if i < 0:
                    value = strip(halo, -1 - i)
                else:
                    value = jnp.where(up, strip(cells, i), strip(cells, rows - 1 - i))
                return jnp.where(wet > 0.0, value, 0.0), wet

            def rates_of(i):
                kinds = facing(classes, i)
                speed = speeds[0]
                for level in range(1, 8):
                    speed = jnp.where(kinds == level, speeds[level], speed)
                return jnp.abs(speed * cosine), jnp.abs(speed * sine)

            def beside(v):
                return jnp.where(eastward, pltpu.roll(v, 1, 1), pltpu.roll(v, window - 1, 1))

            def moved(v, across, zonal, meridional, wet):
                return (v - zonal * (v - beside(v)) - meridional * (v - across)) * wet

            behind, _ = upstream(wanted[0] - 2)
            earlier = None
            for i in range(wanted[0] - 1, wanted[-1] + 1):
                value, wet = upstream(i)
                speed = rates_of(i)
                first = moved(value, behind, *speed, wet)
                behind = value
                if i >= wanted[0]:
                    second = moved(first, earlier, *speed, wet)
                    for t in range(CHUNK // LANE):
                        put(i, t, here, second[:, LANE * t : LANE * (t + 1)], up[:, :LANE])
                earlier = first

        def wait_part(q):
            for k, (low, size) in enumerate(parts):

                @pl.when(q == k)
                def _():
                    part = halo.at[own(low, size)]
                    pltpu.make_async_copy(part, part, halo_recv.at[k]).wait()

        def send_run(ref, base, q, start, count, up, ahead):
            for j in range(comp_count // 2):
                home = jnp.where(up == ahead, comp_count // 2 + j, j)
                source = ref.at[base + home, pl.ds(start, count)]
                place = gathered.at[q, pl.ds(c * comp_local + start, count)]

                @pl.when(home == c)
                def _():
                    pltpu.make_async_copy(source, place, there_recv.at[q]).start()

                @pl.when(home != c)
                def _():
                    pltpu.make_async_remote_copy(
                        src_ref=source,
                        dst_ref=place,
                        send_sem=there_send.at[q],
                        recv_sem=there_recv.at[q],
                        device_id=(home, l),
                        device_id_type=MESH,
                    ).start()

        def by_halves(ref, q, wanted, ahead, first_halo=None):
            base = q * comp_count

            def put(i, t, here, values, up):
                ref[base + i * 2 + t, here, :] = values
                ref[base + (rows - 1 - i) * 2 + t, here, :] = values

            def send_quarter(k):
                @pl.loop(k * quarter, (k + 1) * quarter)
                def _(m):
                    start, up = run_of(m)
                    send_run(ref, base, q, start, RUN, up, ahead)

            done = 0
            for k in range(4):
                need = comp_local if k == 3 else (k + 1) * quarter * RUN + rest
                ready = min(-(-need // (8 * PAIR)), groups // PAIR)

                @pl.loop(done, ready)
                def _(g):
                    for h in range(PAIR):
                        advect_group(q, pl.multiple_of(g * (8 * PAIR) + h * 8, 8), wanted, put)

                done = ready
                if k == 3:
                    for start in tail_groups:
                        advect_group(q, start, wanted, put)
                if first_halo == 0 and k == 0:
                    pl.semaphore_wait(barrier, comp_count + 1)
                send_quarter(k)
                if first_halo is not None and k % 2 == 1:
                    send_halos(first_halo + k // 2)

            send_run(ref, base, q, rest_run[0], rest, rest_run[1], ahead)

        wait_cells(0)
        for q in range(EARLY):
            by_halves(early, q, (2, 3), True, 2 * q if q < EARLY // 2 else None)
        for q in range(EARLY, chunks):
            send_halos(q)
        pltpu.make_async_copy(pair_in, map_in, map_sem.at[0]).start()
        pltpu.make_async_copy(pair_out, map_out, map_sem.at[1]).start()
        for q in range(EARLY):
            wait_part(q)
            by_halves(advected, q, (0, 1), False)

        @pl.loop(EARLY, chunks)
        def _(q):
            wait_part(q)
            held = {}

            def put(i, t, here, values, up):
                held[i, t] = values
                if i >= rows // 2:
                    mirror = held[rows - 1 - i, t]
                    base = q * comp_count + t
                    advected[base + i * 2, here, :] = jnp.where(up, values, mirror)
                    advected[base + (rows - 1 - i) * 2, here, :] = jnp.where(up, mirror, values)

            @pl.loop(0, groups // PAIR)
            def _(g):
                for h in range(PAIR):
                    advect_group(q, pl.multiple_of(g * (8 * PAIR) + h * 8, 8), (0, 1, 2, 3), put)

            for start in tail_groups:
                advect_group(q, start, (0, 1, 2, 3), put)

            place = gathered.at[q, pl.ds(c * comp_local, comp_local)]
            pltpu.make_async_copy(advected.at[q * comp_count + c], place, there_recv.at[q]).start()

            @pl.loop(1, comp_count)
            def _(d):
                home = lax.rem(c + d, comp_count)
                pltpu.make_async_remote_copy(
                    src_ref=advected.at[q * comp_count + home],
                    dst_ref=place,
                    send_sem=there_send.at[q],
                    recv_sem=there_recv.at[q],
                    device_id=(home, l),
                    device_id_type=MESH,
                ).start()

        for i, ref in enumerate((wind_input, whitecap)):
            for low in range(0, total, LANE):
                size = min(LANE, total - low)
                rates_rows[i : i + 1, low : low + size] = ref[pl.ds(low, size)].reshape(1, size)
        rates[...] = rates_rows[...].T

        pltpu.make_async_copy(pair_in, map_in, map_sem.at[0]).wait()
        pltpu.make_async_copy(pair_out, map_out, map_sem.at[1]).wait()

        @pl.loop(0, chunks)
        def _(q):
            pltpu.make_async_copy(gathered.at[q], gathered.at[q], there_recv.at[q]).wait()
            spectra = gathered[q]
            half[...] = spectra.astype(BF16)
            mean_energy = jnp.sum(spectra, axis=0, keepdims=True) * (1.0 / total)
            for low, size in row_tiles:
                projected = jnp.dot(
                    map_in[low : low + size, :], half[...], preferred_element_type=F32
                )
                terms[low : low + size, :] = (
                    projected * gathered[q, low : low + size, :]
                ).astype(BF16)
            for low, size in row_tiles:
                transfer = jnp.dot(
                    map_out[low : low + size, :], terms[...], preferred_element_type=F32
                )
                now = gathered[q, low : low + size, :]
                wind = rates[low : low + size, 0:1]
                white = rates[low : low + size, 1:2]
                gathered[q, low : low + size, :] = now + time_step * (
                    wind * now - white * mean_energy * now + transfer
                )

            place = returned.at[q * (CHUNK // LANE) + lax.rem(c, 2), :, c // 2]
            pltpu.make_async_copy(
                gathered.at[q, pl.ds(c * comp_local, comp_local)], place, back_recv.at[q]
            ).start()

            @pl.loop(1, comp_count)
            def _(d):
                origin = lax.rem(c + d, comp_count)
                pltpu.make_async_remote_copy(
                    src_ref=gathered.at[q, pl.ds(origin * comp_local, comp_local)],
                    dst_ref=place,
                    send_sem=back_send.at[q],
                    recv_sem=back_recv.at[q],
                    device_id=(origin, l),
                    device_id_type=MESH,
                ).start()

        for q in range(chunks):
            pltpu.make_async_copy(gathered.at[q], gathered.at[q], back_recv.at[q]).wait()

        sent = gathered.at[0, pl.ds(0, (comp_count - 1) * comp_local)]
        for q, (low, size) in enumerate(parts):
            pltpu.make_async_copy(sent, sent, there_send.at[q]).wait()
            pltpu.make_async_copy(sent, sent, back_send.at[q]).wait()
            part = halo.at[own(low, size)]
            pltpu.make_async_copy(part, part, halo_send.at[q]).wait()

    return kernel


def write_kernel(tiles):
    def kernel(returned, out, sem):
        copies = [
            pltpu.make_async_copy(
                returned.at[tile], out.at[:, :, pl.ds(tile * LANE, LANE)], sem.at[tile]
            )
            for tile in range(tiles)
        ]
        for copy in copies:
            copy.start()
        for copy in copies:
            copy.wait()

    return kernel


def per_device(energy, sea_mask, depth_class, group_speed, wind_input, whitecap, pair_in, pair_out):
    comp_count = lax.axis_size("comp")
    lat_count = lax.axis_size("lat")
    comp_local, rows, lon = energy.shape
    total = comp_local * comp_count
    chunks = lon // CHUNK
    blocks, tiles = chunks * comp_count, lon // LANE
    anywhere = pl.BlockSpec(memory_space=pl.ANY)
    near = pl.BlockSpec(memory_space=pltpu.VMEM)
    dma = pltpu.SemaphoreType.DMA
    returned = pl.pallas_call(
        make_kernel(comp_count, lat_count, comp_local, rows, lon),
        out_shape=pltpu.VMEM((tiles, comp_local, rows, LANE), F32),
        in_specs=[anywhere] * 5 + [pl.BlockSpec(memory_space=pltpu.SMEM), near, near],
        out_specs=near,
        scratch_shapes=[
            pltpu.VMEM((lon // LANE + 2, rows, comp_local, LANE), F32),
            pltpu.VMEM((lon // LANE + 2, 2, comp_local, LANE), F32),
            pltpu.VMEM((EARLY * comp_count, comp_local, LANE), F32),
            pltpu.VMEM((blocks, comp_local, LANE), F32),
            pltpu.VMEM((chunks, total, LANE), F32),
            pltpu.VMEM((total, total), BF16),
            pltpu.VMEM((total, total), BF16),
            pltpu.VMEM((total, LANE), BF16),
            pltpu.VMEM((total, LANE), BF16),
            pltpu.VMEM((16, lon), jnp.int32),
            pltpu.VMEM((16, lon), jnp.int32),
            pltpu.VMEM((rows + 2 * SUB, chunks * (CHUNK // LANE + 1), 8, LANE), F32),
            pltpu.VMEM((rows + 2 * SUB, chunks * (CHUNK // LANE + 1), 8, LANE), jnp.int32),
            pltpu.VMEM((8, total), F32),
            pltpu.VMEM((total, 8), F32),
            pltpu.VMEM((2, NDIR + 8, LANE), F32),
            dma((chunks,)),
            dma((2,)),
            dma((2,)),
            dma((chunks,)),
            dma((chunks,)),
            dma((chunks,)),
            dma((chunks,)),
            dma((chunks,)),
            dma((chunks,)),
        ],
        compiler_params=pltpu.CompilerParams(
            collective_id=0, has_side_effects=True, vmem_limit_bytes=50 * 2**20
        ),
        cost_estimate=pl.CostEstimate(
            flops=4 * total * total * chunks * LANE, bytes_accessed=24 * 2**20, transcendentals=0
        ),
    )(energy, pair_in, pair_out, sea_mask, depth_class, group_speed.T, wind_input, whitecap)
    return pl.pallas_call(
        write_kernel(tiles),
        out_shape=jax.ShapeDtypeStruct(energy.shape, F32),
        in_specs=[near],
        out_specs=anywhere,
        scratch_shapes=[dma((tiles,))],
        compiler_params=pltpu.CompilerParams(vmem_limit_bytes=8 * 2**20),
    )(returned)


def solution(mesh):
    placed = (P("comp", "lat", None), P(), P(), P(), P(), P(), P(), P())
    return jax.shard_map(
        per_device, mesh=mesh, in_specs=placed, out_specs=P("comp", "lat", None), check_vma=False
    )
```

```python
import math

import jax
import numpy as np
import jax.numpy as jnp
from jax import lax
from jax.experimental import pallas as pl
from jax.experimental.pallas import tpu as pltpu
from jax.sharding import PartitionSpec as P

NDIR = 36
SUB = 2
MESH = pl.DeviceIdType.MESH
F32 = jnp.float32
BF16 = jnp.bfloat16

time_step = 0.5

LANE = 128
CHUNK = 256
RUN = 18
EARLY = 4
PAIR = 2


def sections(lon):
    tiles, step = lon // LANE, CHUNK // LANE
    ends = [0] + [min(step * (q + 1) + 1, tiles) for q in range(lon // CHUNK)]
    return [(low, high - low) for low, high in zip(ends, ends[1:])]


def make_kernel(comp_count, lat_count, comp_local, rows, lon):
    chunks = lon // CHUNK
    total = comp_count * comp_local
    parts = sections(lon)
    tiles = lon // LANE
    spread = CHUNK // LANE + 1
    window = spread * LANE
    groups = comp_local // 8
    runs = comp_local // RUN
    rest = comp_local - runs * RUN
    held_rows = pl.ds(0, comp_local)
    tail_groups = range(groups // PAIR * PAIR * 8, comp_local, 8)
    pieces = [runs * k // 4 for k in range(5)]
    halo_after = {(0, 1): 0, (0, 3): 1, (1, 1): 2, (1, 3): 3}
    row_tiles = [(0, 448), (448, 448), (896, 448), (1344, total - 1344)]

    def kernel(
        energy,
        pair_in,
        pair_out,
        sea_mask,
        depth_class,
        group_speed,
        wind_input,
        whitecap,
        returned,
        cells,
        halo,
        early,
        advected,
        gathered,
        map_in,
        map_out,
        half,
        terms,
        mask_rows,
        class_rows,
        sea,
        classes,
        rates_rows,
        rates,
        trig,
        load_sem,
        fact_sem,
        map_sem,
        halo_send,
        halo_recv,
        there_send,
        there_recv,
        back_send,
        back_recv,
    ):
        c = lax.axis_index("comp")
        l = lax.axis_index("lat")
        odd = lax.rem(c, 2)

        def own(low, size):
            return pl.ds(low + 1, size)

        def load_cells(q):
            low, size = parts[q]
            for tile in range(low, low + size):
                for r in range(rows):
                    pltpu.make_async_copy(
                        energy.at[:, r, pl.ds(tile * LANE, LANE)],
                        cells.at[tile + 1, r, held_rows],
                        load_sem.at[q],
                    ).start()

        def wait_cells(q):
            low, size = parts[q]
            part = cells.at[own(low, size), :, held_rows]
            pltpu.make_async_copy(part, part, load_sem.at[q]).wait()

        lat_rows = lat_count * rows
        fact_low = jnp.clip((l * rows - SUB + 8) // 8 - 1, 0, lat_rows // 8 - 2) * 8
        fact_rows = pl.ds(pl.multiple_of(fact_low, 8), 16)
        fact_copies = [
            pltpu.make_async_copy(sea_mask.at[fact_rows], mask_rows, fact_sem.at[0]),
            pltpu.make_async_copy(depth_class.at[fact_rows], class_rows, fact_sem.at[1]),
        ]
        for copy in fact_copies:
            copy.start()
        load_cells(0)

        barrier = pltpu.get_barrier_semaphore()
        north = lax.rem(l + 1, lat_count)
        south = lax.rem(l + lat_count - 1, lat_count)
        for d in range(1, comp_count):
            pl.semaphore_signal(
                barrier, inc=1, device_id=(lax.rem(c + d, comp_count), l), device_id_type=MESH
            )
        for other in (north, south):
            pl.semaphore_signal(barrier, inc=1, device_id=(c, other), device_id_type=MESH)

        angles = 2.0 * math.pi * (np.arange(trig.shape[1]) % NDIR + 0.5) / NDIR
        for i, values in enumerate((np.cos(angles), np.sin(angles))):
            for j, value in enumerate(values):
                trig[i, j : j + 1, :] = jnp.full((1, LANE), value, F32)

        lane = lax.broadcasted_iota(jnp.int32, (8, LANE), 1)

        def edge(before, after):
            return jnp.where(lane < LANE // 2, after, before)

        for copy in fact_copies:
            copy.wait()
        for i in range(rows + 2 * SUB):
            row = l * rows + i - SUB
            inside = jnp.logical_and(row >= 0, row < lat_rows).astype(jnp.int32)
            at = pl.ds(jnp.clip(row, 0, lat_rows - 1) - fact_low, 1)
            for ref, values in (
                (sea, (mask_rows[at, :] * inside).astype(F32)),
                (classes, class_rows[at, :]),
            ):
                blank = jnp.zeros((8, LANE), values.dtype)
                wide = [
                    jnp.broadcast_to(values[:, k * LANE : (k + 1) * LANE], (8, LANE))
                    for k in range(tiles)
                ]
                wide = [blank] + wide + [blank]
                for q in range(chunks):
                    first = q * (CHUNK // LANE)
                    for t in range(spread - 1):
                        ref[i, q * spread + t] = wide[first + 1 + t]
                    ref[i, q * spread + spread - 1] = edge(wide[first], wide[first + spread])
        for q in range(1, chunks):
            load_cells(q)

        def send_halo(start, count, up, q):
            low, size = parts[q]
            for near in range(2):
                for is_up in (True, False):

                    @pl.when(up if is_up else jnp.logical_not(up))
                    def _():
                        pltpu.make_async_remote_copy(
                            src_ref=cells.at[
                                own(low, size),
                                rows - 1 - near if is_up else near,
                                pl.ds(start, count),
                            ],
                            dst_ref=halo.at[own(low, size), near, pl.ds(start, count)],
                            send_sem=halo_send.at[q],
                            recv_sem=halo_recv.at[q],
                            device_id=(c, north if is_up else south),
                            device_id_type=MESH,
                        ).start()

        def run_of(m):
            return m * RUN + odd * rest, lax.rem((c + odd) // 2 + m, 2) == 0

        rest_run = ((1 - odd) * runs * RUN, lax.rem(c, 4) < 2)

        def send_halos(q):
            if q > 0:
                wait_cells(q)

            @pl.loop(0, runs)
            def _(m):
                start, up = run_of(m)
                send_halo(start, RUN, up, q)

            send_halo(rest_run[0], rest, rest_run[1], q)

        def advect_group(q, start, wanted, put):
            here = pl.ds(start, 8)
            tile = q * (CHUNK // LANE)
            ident = c * comp_local + start
            first_tile = q * spread
            sublane = lax.broadcasted_iota(jnp.int32, (8, LANE), 0)
            low_freq = ident // NDIR
            high_freq = jnp.minimum((ident + 7) // NDIR, group_speed.shape[1] - 1)
            later = sublane + lax.rem(ident, NDIR) >= NDIR

            def wide(v):
                return jnp.concatenate([v] * spread, axis=1)

            angle = pl.ds(lax.rem(ident, NDIR), 8)
            cosine, sine = wide(trig[0, angle, :]), wide(trig[1, angle, :])
            up = sine > 0.0
            eastward = cosine > 0.0
            speeds = [
                wide(jnp.where(later, group_speed[j, high_freq], group_speed[j, low_freq]))
                for j in range(8)
            ]

            def strip(ref, i):
                parts = [ref[tile + t, i, here, :] for t in range(spread + 1)]
                return jnp.concatenate(parts[1:-1] + [edge(parts[0], parts[-1])], axis=1)

            def fact(ref, i):
                return jnp.concatenate([ref[i, first_tile + t] for t in range(spread)], axis=1)

            def facing(ref, i):
                return jnp.where(up, fact(ref, i + SUB), fact(ref, SUB + rows - 1 - i))

            def upstream(i):
                wet = facing(sea, i)
                if i < 0:
                    value = strip(halo, -1 - i)
                else:
                    value = jnp.where(up, strip(cells, i), strip(cells, rows - 1 - i))
                return jnp.where(wet > 0.0, value, 0.0), wet

            def rates_of(i):
                kinds = facing(classes, i)
                speed = speeds[0]
                for level in range(1, 8):
                    speed = jnp.where(kinds == level, speeds[level], speed)
                return jnp.abs(speed * cosine), jnp.abs(speed * sine)

            def beside(v):
                return jnp.where(eastward, pltpu.roll(v, 1, 1), pltpu.roll(v, window - 1, 1))

            def moved(v, across, zonal, meridional, wet):
                return (v - zonal * (v - beside(v)) - meridional * (v - across)) * wet

            behind, _ = upstream(wanted[0] - 2)
            earlier = None
            for i in range(wanted[0] - 1, wanted[-1] + 1):
                value, wet = upstream(i)
                speed = rates_of(i)
                first = moved(value, behind, *speed, wet)
                behind = value
                if i >= wanted[0]:
                    second = moved(first, earlier, *speed, wet)
                    for t in range(CHUNK // LANE):
                        put(i, t, here, second[:, LANE * t : LANE * (t + 1)], up[:, :LANE])
                earlier = first

        def wait_part(q):
            for k, (low, size) in enumerate(parts):

                @pl.when(q == k)
                def _():
                    part = halo.at[own(low, size), :, held_rows]
                    pltpu.make_async_copy(part, part, halo_recv.at[k]).wait()

        def send_run(ref, base, q, start, count, up, ahead):
            for j in range(comp_count // 2):
                home = jnp.where(up == ahead, comp_count // 2 + j, j)
                source = ref.at[base + home, pl.ds(start, count)]
                place = gathered.at[q, pl.ds(c * comp_local + start, count)]

                @pl.when(home == c)
                def _():
                    pltpu.make_async_copy(source, place, there_recv.at[q]).start()

                @pl.when(home != c)
                def _():
                    pltpu.make_async_remote_copy(
                        src_ref=source,
                        dst_ref=place,
                        send_sem=there_send.at[q],
                        recv_sem=there_recv.at[q],
                        device_id=(home, l),
                        device_id_type=MESH,
                    ).start()

        def by_halves(ref, q, wanted, ahead):
            base = q * comp_count

            def put(i, t, here, values, up):
                ref[base + i * 2 + t, here, :] = values
                ref[base + (rows - 1 - i) * 2 + t, here, :] = values

            def send_piece(k):
                @pl.loop(pieces[k], pieces[k + 1])
                def _(m):
                    start, up = run_of(m)
                    send_run(ref, base, q, start, RUN, up, ahead)

            done = 0
            for k in range(4):
                need = comp_local if k == 3 else pieces[k + 1] * RUN + rest
                ready = min(-(-need // (8 * PAIR)), groups // PAIR)

                @pl.loop(done, ready)
                def _(g):
                    for h in range(PAIR):
                        advect_group(q, pl.multiple_of(g * (8 * PAIR) + h * 8, 8), wanted, put)

                done = ready
                if k == 3:
                    for start in tail_groups:
                        advect_group(q, start, wanted, put)
                if ahead and q == 0 and k == 0:
                    pl.semaphore_wait(barrier, comp_count + 1)
                send_piece(k)
                if ahead and (q, k) in halo_after:
                    send_halos(halo_after[q, k])

            send_run(ref, base, q, rest_run[0], rest, rest_run[1], ahead)

        wait_cells(0)
        for q in range(EARLY):
            by_halves(early, q, (2, 3), True)
        for q in range(EARLY, chunks):
            send_halos(q)
        pltpu.make_async_copy(pair_in, map_in, map_sem.at[0]).start()
        pltpu.make_async_copy(pair_out, map_out, map_sem.at[1]).start()
        for q in range(EARLY):
            wait_part(q)
            by_halves(advected, q, (0, 1), False)

        @pl.loop(EARLY, chunks)
        def _(q):
            wait_part(q)
            held = {}

            def put(i, t, here, values, up):
                held[i, t] = values
                if i >= rows // 2:
                    mirror = held[rows - 1 - i, t]
                    base = q * comp_count + t
                    advected[base + i * 2, here, :] = jnp.where(up, values, mirror)
                    advected[base + (rows - 1 - i) * 2, here, :] = jnp.where(up, mirror, values)

            @pl.loop(0, groups // PAIR)
            def _(g):
                for h in range(PAIR):
                    advect_group(q, pl.multiple_of(g * (8 * PAIR) + h * 8, 8), (0, 1, 2, 3), put)

            for start in tail_groups:
                advect_group(q, start, (0, 1, 2, 3), put)

            place = gathered.at[q, pl.ds(c * comp_local, comp_local)]
            pltpu.make_async_copy(
                advected.at[q * comp_count + c, held_rows], place, there_recv.at[q]
            ).start()

            @pl.loop(1, comp_count)
            def _(d):
                home = lax.rem(c + d, comp_count)
                pltpu.make_async_remote_copy(
                    src_ref=advected.at[q * comp_count + home, held_rows],
                    dst_ref=place,
                    send_sem=there_send.at[q],
                    recv_sem=there_recv.at[q],
                    device_id=(home, l),
                    device_id_type=MESH,
                ).start()

        for i, ref in enumerate((wind_input, whitecap)):
            for low in range(0, total, LANE):
                size = min(LANE, total - low)
                rates_rows[i : i + 1, low : low + size] = ref[pl.ds(low, size)].reshape(1, size)
        rates[...] = rates_rows[...].T

        pltpu.make_async_copy(pair_in, map_in, map_sem.at[0]).wait()
        pltpu.make_async_copy(pair_out, map_out, map_sem.at[1]).wait()

        @pl.loop(0, chunks)
        def _(q):
            pltpu.make_async_copy(gathered.at[q], gathered.at[q], there_recv.at[q]).wait()
            spectra = gathered[q]
            half[...] = spectra.astype(BF16)
            mean_energy = jnp.sum(spectra, axis=0, keepdims=True) * (1.0 / total)
            for low, size in row_tiles:
                projected = jnp.dot(
                    map_in[low : low + size, :], half[...], preferred_element_type=F32
                )
                terms[low : low + size, :] = (
                    projected * gathered[q, low : low + size, :]
                ).astype(BF16)
            for low, size in row_tiles:
                transfer = jnp.dot(
                    map_out[low : low + size, :], terms[...], preferred_element_type=F32
                )
                now = gathered[q, low : low + size, :]
                wind = rates[low : low + size, 0:1]
                white = rates[low : low + size, 1:2]
                gathered[q, low : low + size, :] = now + time_step * (
                    wind * now - white * mean_energy * now + transfer
                )

            place = returned.at[q * (CHUNK // LANE) + lax.rem(c, 2), :, c // 2]
            pltpu.make_async_copy(
                gathered.at[q, pl.ds(c * comp_local, comp_local)], place, back_recv.at[q]
            ).start()

            @pl.loop(1, comp_count)
            def _(d):
                origin = lax.rem(c + d, comp_count)
                pltpu.make_async_remote_copy(
                    src_ref=gathered.at[q, pl.ds(origin * comp_local, comp_local)],
                    dst_ref=place,
                    send_sem=back_send.at[q],
                    recv_sem=back_recv.at[q],
                    device_id=(origin, l),
                    device_id_type=MESH,
                ).start()

        for q in range(chunks):
            pltpu.make_async_copy(gathered.at[q], gathered.at[q], back_recv.at[q]).wait()

        sent = gathered.at[0, pl.ds(0, (comp_count - 1) * comp_local)]
        for q, (low, size) in enumerate(parts):
            pltpu.make_async_copy(sent, sent, there_send.at[q]).wait()
            pltpu.make_async_copy(sent, sent, back_send.at[q]).wait()
            part = halo.at[own(low, size), :, held_rows]
            pltpu.make_async_copy(part, part, halo_send.at[q]).wait()

    return kernel


def write_kernel(tiles):
    def kernel(returned, out, sem):
        copies = [
            pltpu.make_async_copy(
                returned.at[tile], out.at[:, :, pl.ds(tile * LANE, LANE)], sem.at[tile]
            )
            for tile in range(tiles)
        ]
        for copy in copies:
            copy.start()
        for copy in copies:
            copy.wait()

    return kernel


def per_device(energy, sea_mask, depth_class, group_speed, wind_input, whitecap, pair_in, pair_out):
    comp_count = lax.axis_size("comp")
    lat_count = lax.axis_size("lat")
    comp_local, rows, lon = energy.shape
    total = comp_local * comp_count
    chunks = lon // CHUNK
    blocks, tiles = chunks * comp_count, lon // LANE
    padded = -(-comp_local // 8) * 8
    anywhere = pl.BlockSpec(memory_space=pl.ANY)
    near = pl.BlockSpec(memory_space=pltpu.VMEM)
    dma = pltpu.SemaphoreType.DMA
    returned = pl.pallas_call(
        make_kernel(comp_count, lat_count, comp_local, rows, lon),
        out_shape=pltpu.VMEM((tiles, comp_local, rows, LANE), F32),
        in_specs=[anywhere] * 5 + [pl.BlockSpec(memory_space=pltpu.SMEM), near, near],
        out_specs=near,
        scratch_shapes=[
            pltpu.VMEM((lon // LANE + 2, rows, padded, LANE), F32),
            pltpu.VMEM((lon // LANE + 2, 2, padded, LANE), F32),
            pltpu.VMEM((EARLY * comp_count, padded, LANE), F32),
            pltpu.VMEM((blocks, padded, LANE), F32),
            pltpu.VMEM((chunks, total, LANE), F32),
            pltpu.VMEM((total, total), BF16),
            pltpu.VMEM((total, total), BF16),
            pltpu.VMEM((total, LANE), BF16),
            pltpu.VMEM((total, LANE), BF16),
            pltpu.VMEM((16, lon), jnp.int32),
            pltpu.VMEM((16, lon), jnp.int32),
            pltpu.VMEM((rows + 2 * SUB, chunks * (CHUNK // LANE + 1), 8, LANE), F32),
            pltpu.VMEM((rows + 2 * SUB, chunks * (CHUNK // LANE + 1), 8, LANE), jnp.int32),
            pltpu.VMEM((8, total), F32),
            pltpu.VMEM((total, 8), F32),
            pltpu.VMEM((2, NDIR + 8, LANE), F32),
            dma((chunks,)),
            dma((2,)),
            dma((2,)),
            dma((chunks,)),
            dma((chunks,)),
            dma((chunks,)),
            dma((chunks,)),
            dma((chunks,)),
            dma((chunks,)),
        ],
        compiler_params=pltpu.CompilerParams(
            collective_id=0, has_side_effects=True, vmem_limit_bytes=50 * 2**20
        ),
        cost_estimate=pl.CostEstimate(
            flops=4 * total * total * chunks * LANE, bytes_accessed=24 * 2**20, transcendentals=0
        ),
    )(energy, pair_in, pair_out, sea_mask, depth_class, group_speed.T, wind_input, whitecap)
    return pl.pallas_call(
        write_kernel(tiles),
        out_shape=jax.ShapeDtypeStruct(energy.shape, F32),
        in_specs=[near],
        out_specs=anywhere,
        scratch_shapes=[dma((tiles,))],
        compiler_params=pltpu.CompilerParams(vmem_limit_bytes=8 * 2**20),
    )(returned)


def solution(mesh):
    placed = (P("comp", "lat", None), P(), P(), P(), P(), P(), P(), P())
    return jax.shard_map(
        per_device, mesh=mesh, in_specs=placed, out_specs=P("comp", "lat", None), check_vma=False
    )
```

```python
import math

import jax
import numpy as np
import jax.numpy as jnp
from jax import lax
from jax.experimental import pallas as pl
from jax.experimental.pallas import tpu as pltpu
from jax.sharding import PartitionSpec as P

NDIR = 36
SUB = 2
MESH = pl.DeviceIdType.MESH
F32 = jnp.float32
BF16 = jnp.bfloat16

time_step = 0.5

LANE = 128
CHUNK = 256
RUN = 18
EARLY = 4
PAIR = 2


def sections(lon):
    tiles, step = lon // LANE, CHUNK // LANE
    ends = [0] + [min(step * (q + 1) + 1, tiles) for q in range(lon // CHUNK)]
    return [(low, high - low) for low, high in zip(ends, ends[1:])]


def make_kernel(comp_count, lat_count, comp_local, rows, lon):
    chunks = lon // CHUNK
    total = comp_count * comp_local
    parts = sections(lon)
    tiles = lon // LANE
    spread = CHUNK // LANE + 1
    window = spread * LANE
    groups = comp_local // 8
    runs = comp_local // RUN
    rest = comp_local - runs * RUN
    held_rows = pl.ds(0, comp_local)
    tail_groups = range(groups // PAIR * PAIR * 8, comp_local, 8)
    pieces = [runs * k // 4 for k in range(5)]
    halo_after = {(0, 1): 0, (0, 3): 1, (1, 1): 2, (1, 3): 3}
    row_tiles = [(0, 448), (448, 448), (896, 448), (1344, total - 1344)]

    def kernel(
        energy,
        pair_in,
        pair_out,
        sea_mask,
        depth_class,
        group_speed,
        wind_input,
        whitecap,
        returned,
        cells,
        halo,
        early,
        advected,
        gathered,
        map_in,
        map_out,
        half,
        terms,
        mask_rows,
        class_rows,
        sea,
        classes,
        rates_rows,
        rates,
        trig,
        load_sem,
        fact_sem,
        map_sem,
        halo_send,
        halo_recv,
        there_send,
        there_recv,
        back_send,
        back_recv,
    ):
        c = lax.axis_index("comp")
        l = lax.axis_index("lat")
        odd = lax.rem(c, 2)

        def own(low, size):
            return pl.ds(low + 1, size)

        def load_cells(q, some=held_rows, sem=None):
            low, size = parts[q]
            for tile in range(low, low + size):
                for r in range(rows):
                    pltpu.make_async_copy(
                        energy.at[some, r, pl.ds(tile * LANE, LANE)],
                        cells.at[tile + 1, r, some],
                        load_sem.at[q if sem is None else sem],
                    ).start()

        def wait_cells(q, some=held_rows, sem=None):
            low, size = parts[q]
            part = cells.at[own(low, size), :, some]
            pltpu.make_async_copy(part, part, load_sem.at[q if sem is None else sem]).wait()

        opening = -(-(pieces[1] * RUN + rest) // (8 * PAIR)) * (8 * PAIR)
        opening_rows, other_rows = pl.ds(0, opening), pl.ds(opening, comp_local - opening)

        barrier = pltpu.get_barrier_semaphore()
        north = lax.rem(l + 1, lat_count)
        south = lax.rem(l + lat_count - 1, lat_count)
        for d in range(1, comp_count):
            pl.semaphore_signal(
                barrier, inc=1, device_id=(lax.rem(c + d, comp_count), l), device_id_type=MESH
            )
        for other in (north, south):
            pl.semaphore_signal(barrier, inc=1, device_id=(c, other), device_id_type=MESH)

        lat_rows = lat_count * rows
        fact_low = jnp.clip((l * rows - SUB + 8) // 8 - 1, 0, lat_rows // 8 - 2) * 8
        fact_rows = pl.ds(pl.multiple_of(fact_low, 8), 16)
        fact_copies = [
            pltpu.make_async_copy(sea_mask.at[fact_rows], mask_rows, fact_sem.at[0]),
            pltpu.make_async_copy(depth_class.at[fact_rows], class_rows, fact_sem.at[1]),
        ]
        for copy in fact_copies:
            copy.start()
        load_cells(0, opening_rows)

        angles = 2.0 * math.pi * (np.arange(trig.shape[1]) % NDIR + 0.5) / NDIR
        for i, values in enumerate((np.cos(angles), np.sin(angles))):
            for j, value in enumerate(values):
                trig[i, j : j + 1, :] = jnp.full((1, LANE), value, F32)

        lane = lax.broadcasted_iota(jnp.int32, (8, LANE), 1)

        def edge(before, after):
            return jnp.where(lane < LANE // 2, after, before)

        for copy in fact_copies:
            copy.wait()
        for i in range(rows + 2 * SUB):
            row = l * rows + i - SUB
            inside = jnp.logical_and(row >= 0, row < lat_rows).astype(jnp.int32)
            at = pl.ds(jnp.clip(row, 0, lat_rows - 1) - fact_low, 1)
            for ref, values in (
                (sea, (mask_rows[at, :] * inside).astype(F32)),
                (classes, class_rows[at, :]),
            ):
                blank = jnp.zeros((8, LANE), values.dtype)
                wide = [
                    jnp.broadcast_to(values[:, k * LANE : (k + 1) * LANE], (8, LANE))
                    for k in range(tiles)
                ]
                wide = [blank] + wide + [blank]
                for q in range(chunks):
                    first = q * (CHUNK // LANE)
                    for t in range(spread - 1):
                        ref[i, q * spread + t] = wide[first + 1 + t]
                    ref[i, q * spread + spread - 1] = edge(wide[first], wide[first + spread])
        load_cells(0, other_rows, chunks)
        for q in range(1, chunks):
            load_cells(q)

        def send_halo(start, count, up, q):
            low, size = parts[q]
            for near in range(2):
                for is_up in (True, False):

                    @pl.when(up if is_up else jnp.logical_not(up))
                    def _():
                        pltpu.make_async_remote_copy(
                            src_ref=cells.at[
                                own(low, size),
                                rows - 1 - near if is_up else near,
                                pl.ds(start, count),
                            ],
                            dst_ref=halo.at[own(low, size), near, pl.ds(start, count)],
                            send_sem=halo_send.at[q],
                            recv_sem=halo_recv.at[q],
                            device_id=(c, north if is_up else south),
                            device_id_type=MESH,
                        ).start()

        def run_of(m):
            return m * RUN + odd * rest, lax.rem((c + odd) // 2 + m, 2) == 0

        rest_run = ((1 - odd) * runs * RUN, lax.rem(c, 4) < 2)

        def send_halos(q):
            if q > 0:
                wait_cells(q)

            @pl.loop(0, runs)
            def _(m):
                start, up = run_of(m)
                send_halo(start, RUN, up, q)

            send_halo(rest_run[0], rest, rest_run[1], q)

        def advect_group(q, start, wanted, put):
            here = pl.ds(start, 8)
            tile = q * (CHUNK // LANE)
            ident = c * comp_local + start
            first_tile = q * spread
            sublane = lax.broadcasted_iota(jnp.int32, (8, LANE), 0)
            low_freq = ident // NDIR
            high_freq = jnp.minimum((ident + 7) // NDIR, group_speed.shape[1] - 1)
            later = sublane + lax.rem(ident, NDIR) >= NDIR

            def wide(v):
                return jnp.concatenate([v] * spread, axis=1)

            angle = pl.ds(lax.rem(ident, NDIR), 8)
            cosine, sine = wide(trig[0, angle, :]), wide(trig[1, angle, :])
            up = sine > 0.0
            eastward = cosine > 0.0
            speeds = [
                wide(jnp.where(later, group_speed[j, high_freq], group_speed[j, low_freq]))
                for j in range(8)
            ]

            def strip(ref, i):
                parts = [ref[tile + t, i, here, :] for t in range(spread + 1)]
                return jnp.concatenate(parts[1:-1] + [edge(parts[0], parts[-1])], axis=1)

            def fact(ref, i):
                return jnp.concatenate([ref[i, first_tile + t] for t in range(spread)], axis=1)

            def facing(ref, i):
                return jnp.where(up, fact(ref, i + SUB), fact(ref, SUB + rows - 1 - i))

            def upstream(i):
                wet = facing(sea, i)
                if i < 0:
                    value = strip(halo, -1 - i)
                else:
                    value = jnp.where(up, strip(cells, i), strip(cells, rows - 1 - i))
                return jnp.where(wet > 0.0, value, 0.0), wet

            def rates_of(i):
                kinds = facing(classes, i)
                speed = speeds[0]
                for level in range(1, 8):
                    speed = jnp.where(kinds == level, speeds[level], speed)
                return jnp.abs(speed * cosine), jnp.abs(speed * sine)

            def beside(v):
                return jnp.where(eastward, pltpu.roll(v, 1, 1), pltpu.roll(v, window - 1, 1))

            def moved(v, across, zonal, meridional, wet):
                return (v - zonal * (v - beside(v)) - meridional * (v - across)) * wet

            behind, _ = upstream(wanted[0] - 2)
            earlier = None
            for i in range(wanted[0] - 1, wanted[-1] + 1):
                value, wet = upstream(i)
                speed = rates_of(i)
                first = moved(value, behind, *speed, wet)
                behind = value
                if i >= wanted[0]:
                    second = moved(first, earlier, *speed, wet)
                    for t in range(CHUNK // LANE):
                        put(i, t, here, second[:, LANE * t : LANE * (t + 1)], up[:, :LANE])
                earlier = first

        def wait_part(q):
            for k, (low, size) in enumerate(parts):

                @pl.when(q == k)
                def _():
                    part = halo.at[own(low, size), :, held_rows]
                    pltpu.make_async_copy(part, part, halo_recv.at[k]).wait()

        def send_run(ref, base, q, start, count, up, ahead):
            for j in range(comp_count // 2):
                home = jnp.where(up == ahead, comp_count // 2 + j, j)
                source = ref.at[base + home, pl.ds(start, count)]
                place = gathered.at[q, pl.ds(c * comp_local + start, count)]

                @pl.when(home == c)
                def _():
                    pltpu.make_async_copy(source, place, there_recv.at[q]).start()

                @pl.when(home != c)
                def _():
                    pltpu.make_async_remote_copy(
                        src_ref=source,
                        dst_ref=place,
                        send_sem=there_send.at[q],
                        recv_sem=there_recv.at[q],
                        device_id=(home, l),
                        device_id_type=MESH,
                    ).start()

        def by_halves(ref, q, wanted, ahead):
            base = q * comp_count

            def put(i, t, here, values, up):
                ref[base + i * 2 + t, here, :] = values
                ref[base + (rows - 1 - i) * 2 + t, here, :] = values

            def send_piece(k):
                @pl.loop(pieces[k], pieces[k + 1])
                def _(m):
                    start, up = run_of(m)
                    send_run(ref, base, q, start, RUN, up, ahead)

            done = 0
            for k in range(4):
                need = comp_local if k == 3 else pieces[k + 1] * RUN + rest
                ready = min(-(-need // (8 * PAIR)), groups // PAIR)

                @pl.loop(done, ready)
                def _(g):
                    for h in range(PAIR):
                        advect_group(q, pl.multiple_of(g * (8 * PAIR) + h * 8, 8), wanted, put)

                done = ready
                if k == 3:
                    for start in tail_groups:
                        advect_group(q, start, wanted, put)
                if ahead and q == 0 and k == 0:
                    pl.semaphore_wait(barrier, comp_count + 1)
                send_piece(k)
                if ahead and q == 0 and k == 0:
                    wait_cells(0, other_rows, chunks)
                if ahead and (q, k) in halo_after:
                    send_halos(halo_after[q, k])

            send_run(ref, base, q, rest_run[0], rest, rest_run[1], ahead)

        wait_cells(0, opening_rows)
        for q in range(EARLY):
            by_halves(early, q, (2, 3), True)
        for q in range(EARLY, chunks):
            send_halos(q)
        pltpu.make_async_copy(pair_in, map_in, map_sem.at[0]).start()
        pltpu.make_async_copy(pair_out, map_out, map_sem.at[1]).start()
        for q in range(EARLY):
            wait_part(q)
            by_halves(advected, q, (0, 1), False)

        @pl.loop(EARLY, chunks)
        def _(q):
            wait_part(q)
            held = {}

            def put(i, t, here, values, up):
                held[i, t] = values
                if i >= rows // 2:
                    mirror = held[rows - 1 - i, t]
                    base = q * comp_count + t
                    advected[base + i * 2, here, :] = jnp.where(up, values, mirror)
                    advected[base + (rows - 1 - i) * 2, here, :] = jnp.where(up, mirror, values)

            @pl.loop(0, groups // PAIR)
            def _(g):
                for h in range(PAIR):
                    advect_group(q, pl.multiple_of(g * (8 * PAIR) + h * 8, 8), (0, 1, 2, 3), put)

            for start in tail_groups:
                advect_group(q, start, (0, 1, 2, 3), put)

            place = gathered.at[q, pl.ds(c * comp_local, comp_local)]
            pltpu.make_async_copy(
                advected.at[q * comp_count + c, held_rows], place, there_recv.at[q]
            ).start()

            @pl.loop(1, comp_count)
            def _(d):
                home = lax.rem(c + d, comp_count)
                pltpu.make_async_remote_copy(
                    src_ref=advected.at[q * comp_count + home, held_rows],
                    dst_ref=place,
                    send_sem=there_send.at[q],
                    recv_sem=there_recv.at[q],
                    device_id=(home, l),
                    device_id_type=MESH,
                ).start()

        for i, ref in enumerate((wind_input, whitecap)):
            for low in range(0, total, LANE):
                size = min(LANE, total - low)
                rates_rows[i : i + 1, low : low + size] = ref[pl.ds(low, size)].reshape(1, size)
        rates[...] = rates_rows[...].T

        pltpu.make_async_copy(pair_in, map_in, map_sem.at[0]).wait()
        pltpu.make_async_copy(pair_out, map_out, map_sem.at[1]).wait()

        @pl.loop(0, chunks)
        def _(q):
            pltpu.make_async_copy(gathered.at[q], gathered.at[q], there_recv.at[q]).wait()
            spectra = gathered[q]
            half[...] = spectra.astype(BF16)
            mean_energy = jnp.sum(spectra, axis=0, keepdims=True) * (1.0 / total)
            for low, size in row_tiles:
                projected = jnp.dot(
                    map_in[low : low + size, :], half[...], preferred_element_type=F32
                )
                terms[low : low + size, :] = (
                    projected * gathered[q, low : low + size, :]
                ).astype(BF16)
            for low, size in row_tiles:
                transfer = jnp.dot(
                    map_out[low : low + size, :], terms[...], preferred_element_type=F32
                )
                now = gathered[q, low : low + size, :]
                wind = rates[low : low + size, 0:1]
                white = rates[low : low + size, 1:2]
                gathered[q, low : low + size, :] = now + time_step * (
                    wind * now - white * mean_energy * now + transfer
                )

            place = returned.at[q * (CHUNK // LANE) + lax.rem(c, 2), :, c // 2]
            pltpu.make_async_copy(
                gathered.at[q, pl.ds(c * comp_local, comp_local)], place, back_recv.at[q]
            ).start()

            @pl.loop(1, comp_count)
            def _(d):
                origin = lax.rem(c + d, comp_count)
                pltpu.make_async_remote_copy(
                    src_ref=gathered.at[q, pl.ds(origin * comp_local, comp_local)],
                    dst_ref=place,
                    send_sem=back_send.at[q],
                    recv_sem=back_recv.at[q],
                    device_id=(origin, l),
                    device_id_type=MESH,
                ).start()

        for q in range(chunks):
            pltpu.make_async_copy(gathered.at[q], gathered.at[q], back_recv.at[q]).wait()

        sent = gathered.at[0, pl.ds(0, (comp_count - 1) * comp_local)]
        for q, (low, size) in enumerate(parts):
            pltpu.make_async_copy(sent, sent, there_send.at[q]).wait()
            pltpu.make_async_copy(sent, sent, back_send.at[q]).wait()
            part = halo.at[own(low, size), :, held_rows]
            pltpu.make_async_copy(part, part, halo_send.at[q]).wait()

    return kernel


def write_kernel(tiles):
    def kernel(returned, out, sem):
        copies = [
            pltpu.make_async_copy(
                returned.at[tile], out.at[:, :, pl.ds(tile * LANE, LANE)], sem.at[tile]
            )
            for tile in range(tiles)
        ]
        for copy in copies:
            copy.start()
        for copy in copies:
            copy.wait()

    return kernel


def per_device(energy, sea_mask, depth_class, group_speed, wind_input, whitecap, pair_in, pair_out):
    comp_count = lax.axis_size("comp")
    lat_count = lax.axis_size("lat")
    comp_local, rows, lon = energy.shape
    total = comp_local * comp_count
    chunks = lon // CHUNK
    blocks, tiles = chunks * comp_count, lon // LANE
    padded = -(-comp_local // 8) * 8
    anywhere = pl.BlockSpec(memory_space=pl.ANY)
    near = pl.BlockSpec(memory_space=pltpu.VMEM)
    dma = pltpu.SemaphoreType.DMA
    returned = pl.pallas_call(
        make_kernel(comp_count, lat_count, comp_local, rows, lon),
        out_shape=pltpu.VMEM((tiles, comp_local, rows, LANE), F32),
        in_specs=[anywhere] * 5 + [pl.BlockSpec(memory_space=pltpu.SMEM), near, near],
        out_specs=near,
        scratch_shapes=[
            pltpu.VMEM((lon // LANE + 2, rows, padded, LANE), F32),
            pltpu.VMEM((lon // LANE + 2, 2, padded, LANE), F32),
            pltpu.VMEM((EARLY * comp_count, padded, LANE), F32),
            pltpu.VMEM((blocks, padded, LANE), F32),
            pltpu.VMEM((chunks, total, LANE), F32),
            pltpu.VMEM((total, total), BF16),
            pltpu.VMEM((total, total), BF16),
            pltpu.VMEM((total, LANE), BF16),
            pltpu.VMEM((total, LANE), BF16),
            pltpu.VMEM((16, lon), jnp.int32),
            pltpu.VMEM((16, lon), jnp.int32),
            pltpu.VMEM((rows + 2 * SUB, chunks * (CHUNK // LANE + 1), 8, LANE), F32),
            pltpu.VMEM((rows + 2 * SUB, chunks * (CHUNK // LANE + 1), 8, LANE), jnp.int32),
            pltpu.VMEM((8, total), F32),
            pltpu.VMEM((total, 8), F32),
            pltpu.VMEM((2, NDIR + 8, LANE), F32),
            dma((chunks + 1,)),
            dma((2,)),
            dma((2,)),
            dma((chunks,)),
            dma((chunks,)),
            dma((chunks,)),
            dma((chunks,)),
            dma((chunks,)),
            dma((chunks,)),
        ],
        compiler_params=pltpu.CompilerParams(
            collective_id=0, has_side_effects=True, vmem_limit_bytes=50 * 2**20
        ),
        cost_estimate=pl.CostEstimate(
            flops=4 * total * total * chunks * LANE, bytes_accessed=24 * 2**20, transcendentals=0
        ),
    )(energy, pair_in, pair_out, sea_mask, depth_class, group_speed.T, wind_input, whitecap)
    return pl.pallas_call(
        write_kernel(tiles),
        out_shape=jax.ShapeDtypeStruct(energy.shape, F32),
        in_specs=[near],
        out_specs=anywhere,
        scratch_shapes=[dma((tiles,))],
        compiler_params=pltpu.CompilerParams(vmem_limit_bytes=8 * 2**20),
    )(returned)


def solution(mesh):
    placed = (P("comp", "lat", None), P(), P(), P(), P(), P(), P(), P())
    return jax.shard_map(
        per_device, mesh=mesh, in_specs=placed, out_specs=P("comp", "lat", None), check_vma=False
    )
```

```python
import math

import jax
import numpy as np
import jax.numpy as jnp
from jax import lax
from jax.experimental import pallas as pl
from jax.experimental.pallas import tpu as pltpu
from jax.sharding import PartitionSpec as P

NDIR = 36
SUB = 2
MESH = pl.DeviceIdType.MESH
F32 = jnp.float32
BF16 = jnp.bfloat16

time_step = 0.5

LANE = 128
CHUNK = 256
RUN = 18
EARLY = 4
PAIR = 4


def sections(lon):
    tiles, step = lon // LANE, CHUNK // LANE
    ends = [0] + [min(step * (q + 1) + 1, tiles) for q in range(lon // CHUNK)]
    return [(low, high - low) for low, high in zip(ends, ends[1:])]


def make_kernel(comp_count, lat_count, comp_local, rows, lon):
    chunks = lon // CHUNK
    total = comp_count * comp_local
    parts = sections(lon)
    tiles = lon // LANE
    spread = CHUNK // LANE + 1
    window = spread * LANE
    groups = comp_local // 8
    runs = comp_local // RUN
    rest = comp_local - runs * RUN
    held_rows = pl.ds(0, comp_local)
    tail_groups = range(groups // PAIR * PAIR * 8, comp_local, 8)
    pieces = [runs * k // 4 for k in range(5)]
    halo_after = {(0, 1): 0, (0, 3): 1, (1, 1): 2, (1, 3): 3}
    row_tiles = [(0, 448), (448, 448), (896, 448), (1344, total - 1344)]

    def kernel(
        energy,
        pair_in,
        pair_out,
        sea_mask,
        depth_class,
        group_speed,
        wind_input,
        whitecap,
        returned,
        cells,
        halo,
        early,
        advected,
        gathered,
        map_in,
        map_out,
        half,
        terms,
        mask_rows,
        class_rows,
        sea,
        classes,
        rates_rows,
        rates,
        trig,
        load_sem,
        fact_sem,
        map_sem,
        halo_send,
        halo_recv,
        there_send,
        there_recv,
        back_send,
        back_recv,
    ):
        c = lax.axis_index("comp")
        l = lax.axis_index("lat")
        odd = lax.rem(c, 2)

        def own(low, size):
            return pl.ds(low + 1, size)

        def load_cells(q):
            low, size = parts[q]
            for tile in range(low, low + size):
                for r in range(rows):
                    pltpu.make_async_copy(
                        energy.at[:, r, pl.ds(tile * LANE, LANE)],
                        cells.at[tile + 1, r, held_rows],
                        load_sem.at[q],
                    ).start()

        def wait_cells(q):
            low, size = parts[q]
            part = cells.at[own(low, size), :, held_rows]
            pltpu.make_async_copy(part, part, load_sem.at[q]).wait()

        lat_rows = lat_count * rows
        fact_low = jnp.clip((l * rows - SUB + 8) // 8 - 1, 0, lat_rows // 8 - 2) * 8
        fact_rows = pl.ds(pl.multiple_of(fact_low, 8), 16)
        fact_copies = [
            pltpu.make_async_copy(sea_mask.at[fact_rows], mask_rows, fact_sem.at[0]),
            pltpu.make_async_copy(depth_class.at[fact_rows], class_rows, fact_sem.at[1]),
        ]
        for copy in fact_copies:
            copy.start()
        load_cells(0)

        barrier = pltpu.get_barrier_semaphore()
        north = lax.rem(l + 1, lat_count)
        south = lax.rem(l + lat_count - 1, lat_count)
        for d in range(1, comp_count):
            pl.semaphore_signal(
                barrier, inc=1, device_id=(lax.rem(c + d, comp_count), l), device_id_type=MESH
            )
        for other in (north, south):
            pl.semaphore_signal(barrier, inc=1, device_id=(c, other), device_id_type=MESH)

        angles = 2.0 * math.pi * (np.arange(trig.shape[1]) % NDIR + 0.5) / NDIR
        for i, values in enumerate((np.cos(angles), np.sin(angles))):
            for j, value in enumerate(values):
                trig[i, j : j + 1, :] = jnp.full((1, LANE), value, F32)

        lane = lax.broadcasted_iota(jnp.int32, (8, LANE), 1)

        def edge(before, after):
            return jnp.where(lane < LANE // 2, after, before)

        for copy in fact_copies:
            copy.wait()
        for i in range(rows + 2 * SUB):
            row = l * rows + i - SUB
            inside = jnp.logical_and(row >= 0, row < lat_rows).astype(jnp.int32)
            at = pl.ds(jnp.clip(row, 0, lat_rows - 1) - fact_low, 1)
            for ref, values in (
                (sea, (mask_rows[at, :] * inside).astype(F32)),
                (classes, class_rows[at, :]),
            ):
                blank = jnp.zeros((8, LANE), values.dtype)
                wide = [
                    jnp.broadcast_to(values[:, k * LANE : (k + 1) * LANE], (8, LANE))
                    for k in range(tiles)
                ]
                wide = [blank] + wide + [blank]
                for q in range(chunks):
                    first = q * (CHUNK // LANE)
                    for t in range(spread - 1):
                        ref[i, q * spread + t] = wide[first + 1 + t]
                    ref[i, q * spread + spread - 1] = edge(wide[first], wide[first + spread])
        for q in range(1, chunks):
            load_cells(q)

        def send_halo(start, count, up, q):
            low, size = parts[q]
            for near in range(2):
                for is_up in (True, False):

                    @pl.when(up if is_up else jnp.logical_not(up))
                    def _():
                        pltpu.make_async_remote_copy(
                            src_ref=cells.at[
                                own(low, size),
                                rows - 1 - near if is_up else near,
                                pl.ds(start, count),
                            ],
                            dst_ref=halo.at[own(low, size), near, pl.ds(start, count)],
                            send_sem=halo_send.at[q],
                            recv_sem=halo_recv.at[q],
                            device_id=(c, north if is_up else south),
                            device_id_type=MESH,
                        ).start()

        def run_of(m):
            return m * RUN + odd * rest, lax.rem((c + odd) // 2 + m, 2) == 0

        rest_run = ((1 - odd) * runs * RUN, lax.rem(c, 4) < 2)

        def send_halos(q):
            if q > 0:
                wait_cells(q)

            @pl.loop(0, runs)
            def _(m):
                start, up = run_of(m)
                send_halo(start, RUN, up, q)

            send_halo(rest_run[0], rest, rest_run[1], q)

        def advect_group(q, start, wanted, put):
            here = pl.ds(start, 8)
            tile = q * (CHUNK // LANE)
            ident = c * comp_local + start
            first_tile = q * spread
            sublane = lax.broadcasted_iota(jnp.int32, (8, LANE), 0)
            low_freq = ident // NDIR
            high_freq = jnp.minimum((ident + 7) // NDIR, group_speed.shape[1] - 1)
            later = sublane + lax.rem(ident, NDIR) >= NDIR

            def wide(v):
                return jnp.concatenate([v] * spread, axis=1)

            angle = pl.ds(lax.rem(ident, NDIR), 8)
            cosine, sine = wide(trig[0, angle, :]), wide(trig[1, angle, :])
            up = sine > 0.0
            eastward = cosine > 0.0
            speeds = [
                wide(jnp.where(later, group_speed[j, high_freq], group_speed[j, low_freq]))
                for j in range(8)
            ]

            def strip(ref, i):
                parts = [ref[tile + t, i, here, :] for t in range(spread + 1)]
                return jnp.concatenate(parts[1:-1] + [edge(parts[0], parts[-1])], axis=1)

            def fact(ref, i):
                return jnp.concatenate([ref[i, first_tile + t] for t in range(spread)], axis=1)

            def facing(ref, i):
                return jnp.where(up, fact(ref, i + SUB), fact(ref, SUB + rows - 1 - i))

            def upstream(i):
                wet = facing(sea, i)
                if i < 0:
                    value = strip(halo, -1 - i)
                else:
                    value = jnp.where(up, strip(cells, i), strip(cells, rows - 1 - i))
                return jnp.where(wet > 0.0, value, 0.0), wet

            def rates_of(i):
                kinds = facing(classes, i)
                speed = speeds[0]
                for level in range(1, 8):
                    speed = jnp.where(kinds == level, speeds[level], speed)
                return jnp.abs(speed * cosine), jnp.abs(speed * sine)

            def beside(v):
                return jnp.where(eastward, pltpu.roll(v, 1, 1), pltpu.roll(v, window - 1, 1))

            def moved(v, across, zonal, meridional, wet):
                return (v - zonal * (v - beside(v)) - meridional * (v - across)) * wet

            behind, _ = upstream(wanted[0] - 2)
            earlier = None
            for i in range(wanted[0] - 1, wanted[-1] + 1):
                value, wet = upstream(i)
                speed = rates_of(i)
                first = moved(value, behind, *speed, wet)
                behind = value
                if i >= wanted[0]:
                    second = moved(first, earlier, *speed, wet)
                    for t in range(CHUNK // LANE):
                        put(i, t, here, second[:, LANE * t : LANE * (t + 1)], up[:, :LANE])
                earlier = first

        def wait_part(q):
            for k, (low, size) in enumerate(parts):

                @pl.when(q == k)
                def _():
                    part = halo.at[own(low, size), :, held_rows]
                    pltpu.make_async_copy(part, part, halo_recv.at[k]).wait()

        def send_run(ref, base, q, start, count, up, ahead):
            for j in range(comp_count // 2):
                home = jnp.where(up == ahead, comp_count // 2 + j, j)
                source = ref.at[base + home, pl.ds(start, count)]
                place = gathered.at[q, pl.ds(c * comp_local + start, count)]

                @pl.when(home == c)
                def _():
                    pltpu.make_async_copy(source, place, there_recv.at[q]).start()

                @pl.when(home != c)
                def _():
                    pltpu.make_async_remote_copy(
                        src_ref=source,
                        dst_ref=place,
                        send_sem=there_send.at[q],
                        recv_sem=there_recv.at[q],
                        device_id=(home, l),
                        device_id_type=MESH,
                    ).start()

        def by_halves(ref, q, wanted, ahead):
            base = q * comp_count

            def put(i, t, here, values, up):
                ref[base + i * 2 + t, here, :] = values
                ref[base + (rows - 1 - i) * 2 + t, here, :] = values

            def send_piece(k):
                @pl.loop(pieces[k], pieces[k + 1])
                def _(m):
                    start, up = run_of(m)
                    send_run(ref, base, q, start, RUN, up, ahead)

            done = 0
            for k in range(4):
                need = comp_local if k == 3 else pieces[k + 1] * RUN + rest
                ready = min(-(-need // (8 * PAIR)), groups // PAIR)

                @pl.loop(done, ready)
                def _(g):
                    for h in range(PAIR):
                        advect_group(q, pl.multiple_of(g * (8 * PAIR) + h * 8, 8), wanted, put)

                done = ready
                if k == 3:
                    for start in tail_groups:
                        advect_group(q, start, wanted, put)
                if ahead and q == 0 and k == 0:
                    pl.semaphore_wait(barrier, comp_count + 1)
                send_piece(k)
                if ahead and (q, k) in halo_after:
                    send_halos(halo_after[q, k])

            send_run(ref, base, q, rest_run[0], rest, rest_run[1], ahead)

        wait_cells(0)
        for q in range(EARLY):
            by_halves(early, q, (2, 3), True)
        for q in range(EARLY, chunks):
            send_halos(q)
        pltpu.make_async_copy(pair_in, map_in, map_sem.at[0]).start()
        pltpu.make_async_copy(pair_out, map_out, map_sem.at[1]).start()
        for q in range(EARLY):
            wait_part(q)
            by_halves(advected, q, (0, 1), False)

        @pl.loop(EARLY, chunks)
        def _(q):
            wait_part(q)
            held = {}

            def put(i, t, here, values, up):
                held[i, t] = values
                if i >= rows // 2:
                    mirror = held[rows - 1 - i, t]
                    base = q * comp_count + t
                    advected[base + i * 2, here, :] = jnp.where(up, values, mirror)
                    advected[base + (rows - 1 - i) * 2, here, :] = jnp.where(up, mirror, values)

            @pl.loop(0, groups // PAIR)
            def _(g):
                for h in range(PAIR):
                    advect_group(q, pl.multiple_of(g * (8 * PAIR) + h * 8, 8), (0, 1, 2, 3), put)

            for start in tail_groups:
                advect_group(q, start, (0, 1, 2, 3), put)

            place = gathered.at[q, pl.ds(c * comp_local, comp_local)]
            pltpu.make_async_copy(
                advected.at[q * comp_count + c, held_rows], place, there_recv.at[q]
            ).start()

            @pl.loop(1, comp_count)
            def _(d):
                home = lax.rem(c + d, comp_count)
                pltpu.make_async_remote_copy(
                    src_ref=advected.at[q * comp_count + home, held_rows],
                    dst_ref=place,
                    send_sem=there_send.at[q],
                    recv_sem=there_recv.at[q],
                    device_id=(home, l),
                    device_id_type=MESH,
                ).start()

        for i, ref in enumerate((wind_input, whitecap)):
            for low in range(0, total, LANE):
                size = min(LANE, total - low)
                rates_rows[i : i + 1, low : low + size] = ref[pl.ds(low, size)].reshape(1, size)
        rates[...] = rates_rows[...].T

        pltpu.make_async_copy(pair_in, map_in, map_sem.at[0]).wait()
        pltpu.make_async_copy(pair_out, map_out, map_sem.at[1]).wait()

        @pl.loop(0, chunks)
        def _(q):
            pltpu.make_async_copy(gathered.at[q], gathered.at[q], there_recv.at[q]).wait()
            spectra = gathered[q]
            half[...] = spectra.astype(BF16)
            mean_energy = jnp.sum(spectra, axis=0, keepdims=True) * (1.0 / total)
            for low, size in row_tiles:
                projected = jnp.dot(
                    map_in[low : low + size, :], half[...], preferred_element_type=F32
                )
                terms[low : low + size, :] = (
                    projected * gathered[q, low : low + size, :]
                ).astype(BF16)
            for low, size in row_tiles:
                transfer = jnp.dot(
                    map_out[low : low + size, :], terms[...], preferred_element_type=F32
                )
                now = gathered[q, low : low + size, :]
                wind = rates[low : low + size, 0:1]
                white = rates[low : low + size, 1:2]
                gathered[q, low : low + size, :] = now + time_step * (
                    wind * now - white * mean_energy * now + transfer
                )

            place = returned.at[q * (CHUNK // LANE) + lax.rem(c, 2), :, c // 2]
            pltpu.make_async_copy(
                gathered.at[q, pl.ds(c * comp_local, comp_local)], place, back_recv.at[q]
            ).start()

            @pl.loop(1, comp_count)
            def _(d):
                origin = lax.rem(c + d, comp_count)
                pltpu.make_async_remote_copy(
                    src_ref=gathered.at[q, pl.ds(origin * comp_local, comp_local)],
                    dst_ref=place,
                    send_sem=back_send.at[q],
                    recv_sem=back_recv.at[q],
                    device_id=(origin, l),
                    device_id_type=MESH,
                ).start()

        for q in range(chunks):
            pltpu.make_async_copy(gathered.at[q], gathered.at[q], back_recv.at[q]).wait()

        sent = gathered.at[0, pl.ds(0, (comp_count - 1) * comp_local)]
        for q, (low, size) in enumerate(parts):
            pltpu.make_async_copy(sent, sent, there_send.at[q]).wait()
            pltpu.make_async_copy(sent, sent, back_send.at[q]).wait()
            part = halo.at[own(low, size), :, held_rows]
            pltpu.make_async_copy(part, part, halo_send.at[q]).wait()

    return kernel


def write_kernel(tiles):
    def kernel(returned, out, sem):
        copies = [
            pltpu.make_async_copy(
                returned.at[tile], out.at[:, :, pl.ds(tile * LANE, LANE)], sem.at[tile]
            )
            for tile in range(tiles)
        ]
        for copy in copies:
            copy.start()
        for copy in copies:
            copy.wait()

    return kernel


def per_device(energy, sea_mask, depth_class, group_speed, wind_input, whitecap, pair_in, pair_out):
    comp_count = lax.axis_size("comp")
    lat_count = lax.axis_size("lat")
    comp_local, rows, lon = energy.shape
    total = comp_local * comp_count
    chunks = lon // CHUNK
    blocks, tiles = chunks * comp_count, lon // LANE
    padded = -(-comp_local // 8) * 8
    anywhere = pl.BlockSpec(memory_space=pl.ANY)
    near = pl.BlockSpec(memory_space=pltpu.VMEM)
    dma = pltpu.SemaphoreType.DMA
    returned = pl.pallas_call(
        make_kernel(comp_count, lat_count, comp_local, rows, lon),
        out_shape=pltpu.VMEM((tiles, comp_local, rows, LANE), F32),
        in_specs=[anywhere] * 5 + [pl.BlockSpec(memory_space=pltpu.SMEM), near, near],
        out_specs=near,
        scratch_shapes=[
            pltpu.VMEM((lon // LANE + 2, rows, padded, LANE), F32),
            pltpu.VMEM((lon // LANE + 2, 2, padded, LANE), F32),
            pltpu.VMEM((EARLY * comp_count, padded, LANE), F32),
            pltpu.VMEM((blocks, padded, LANE), F32),
            pltpu.VMEM((chunks, total, LANE), F32),
            pltpu.VMEM((total, total), BF16),
            pltpu.VMEM((total, total), BF16),
            pltpu.VMEM((total, LANE), BF16),
            pltpu.VMEM((total, LANE), BF16),
            pltpu.VMEM((16, lon), jnp.int32),
            pltpu.VMEM((16, lon), jnp.int32),
            pltpu.VMEM((rows + 2 * SUB, chunks * (CHUNK // LANE + 1), 8, LANE), F32),
            pltpu.VMEM((rows + 2 * SUB, chunks * (CHUNK // LANE + 1), 8, LANE), jnp.int32),
            pltpu.VMEM((8, total), F32),
            pltpu.VMEM((total, 8), F32),
            pltpu.VMEM((2, NDIR + 8, LANE), F32),
            dma((chunks,)),
            dma((2,)),
            dma((2,)),
            dma((chunks,)),
            dma((chunks,)),
            dma((chunks,)),
            dma((chunks,)),
            dma((chunks,)),
            dma((chunks,)),
        ],
        compiler_params=pltpu.CompilerParams(
            collective_id=0, has_side_effects=True, vmem_limit_bytes=50 * 2**20
        ),
        cost_estimate=pl.CostEstimate(
            flops=4 * total * total * chunks * LANE, bytes_accessed=24 * 2**20, transcendentals=0
        ),
    )(energy, pair_in, pair_out, sea_mask, depth_class, group_speed.T, wind_input, whitecap)
    return pl.pallas_call(
        write_kernel(tiles),
        out_shape=jax.ShapeDtypeStruct(energy.shape, F32),
        in_specs=[near],
        out_specs=anywhere,
        scratch_shapes=[dma((tiles,))],
        compiler_params=pltpu.CompilerParams(vmem_limit_bytes=8 * 2**20),
    )(returned)


def solution(mesh):
    placed = (P("comp", "lat", None), P(), P(), P(), P(), P(), P(), P())
    return jax.shard_map(
        per_device, mesh=mesh, in_specs=placed, out_specs=P("comp", "lat", None), check_vma=False
    )
```
